256 devices in a mesh: grp: 4 (over y), sub: 64 (over x, z, core).
Axes of the slice: x: 4, y: 4, z: 8, core: 2. Of those that a mesh axis runs over, the one named last changes fastest.
Arguments:
- coords: bfloat16 [3, 524288], P(None, ('grp', 'sub')), may hold values from -6 to 6
- rhs: bfloat16 [32, 524288], P(None, ('grp', 'sub')), may hold values from -6 to 6
- leaf_basis: bfloat16 [64, 524288], P(None, ('grp', 'sub')), may hold values from -0.375 to 0.375
- low_transfer: bfloat16 [3584, 64, 64], P(('grp', 'sub')), may hold values from -0.5 to 0.5
- low_pairs: int32 [2, 8192], P(None, ('grp', 'sub')), may hold values from 0 to 3583, as said below
- low_blocks: bfloat16 [8192, 64, 64], P(('grp', 'sub')), may hold values from -0.75 to 0.75
- upper_transfer: bfloat16 [510, 64, 64], replicated, may hold values from -0.5 to 0.5
- upper_pairs: int32 [2, 2048], P(None, ('grp', 'sub')), may hold values from 0 to 509, as said below
- upper_blocks: bfloat16 [2048, 64, 64], P(('grp', 'sub')), may hold values from -0.75 to 0.75
- near_pairs: int32 [2, 20480], P(None, ('grp', 'sub')), may hold values from 0 to 2047, as said below
- near_count: int32 [256], P(('grp', 'sub')), may hold values from 13 to 80, as said below
Outputs:
- potential: float32 [32, 524288], P(None, ('grp', 'sub'))
The draws below stay inside these ranges and needn't reach their ends.
Inputs may be any that keep to these rules, and one draw needn't show every extreme that they name: `near_pairs`: row 0 of column k names a leaf of device k // 80; row 1 names a leaf of that device or of the devices just before and after it in tree order, in every column, used or not. `near_count`: entry d counts the leading used columns among device d's 80 columns of near_pairs; some device uses all 80. `low_pairs`: cluster i of level h of device d has number d * 14 + 2 * 8 - 2 * (8 >> h) + i. The target of column k belongs to device k // 32; its source lies on the same level, on that device or on the device just before or after it. `upper_pairs`: upper cluster i of level j has number 2 * 256 - 2 * (256 >> j) + i. Target and source of a column lie on one level below the top and differ.
All inputs are finite; a program needn't handle non-finite values.
Results may differ from the reference program's by a relative error of at most 0.0029.
Values may be sent and summed in bfloat16 or wider, within the bound.
A program may use at most 128 MiB of HBM per device.

```python
import jax
import jax.numpy as jnp
from jax import lax

LEAF = 256
RANK = 64
NVEC = 32
LEAVES_DEV = 8
UP_DEV = 8
NDEV = 256
NLEAVES = 2048
NPTS = 524288
LOWCL = 14
NEAR_CAP = 80
LOW_DEV = 32


def draw_coords(key, part):
    leaf_id = (jnp.arange(NPTS, dtype=jnp.int32) // LEAF).astype(jnp.float32)
    slopes = jnp.array([0.0011, 0.0017, 0.0023], jnp.float32)[:, None]
    phases = jnp.array([0.1, 0.5, 0.9], jnp.float32)[:, None]
    folded = jnp.mod(leaf_id[None, :] * slopes + phases, 2.0)
    centre = 4.0 * (2.0 * jnp.abs(folded - 1.0) - 1.0)
    jitter = jax.random.uniform(key, (3, NLEAVES, LEAF), jnp.float32, -0.75, 0.75)
    return (centre + jitter.reshape(3, NPTS)).astype(jnp.bfloat16)


def draw_near_pairs(key, part):
    key_target, key_offset = jax.random.split(jax.random.fold_in(key, 11))
    total_slots = NDEV * NEAR_CAP
    slot_dev = jnp.arange(total_slots, dtype=jnp.int32) // NEAR_CAP
    targets = slot_dev * LEAVES_DEV + jax.random.randint(key_target, (total_slots,), 0, LEAVES_DEV, dtype=jnp.int32)
    offsets = jax.random.randint(key_offset, (total_slots,), -LEAVES_DEV, LEAVES_DEV + 1, dtype=jnp.int32)
    sources = jnp.clip(targets + offsets, 0, NLEAVES - 1)
    return jnp.stack([targets, sources])


def draw_near_count(key, part):
    key_heavy, key_light, key_busy, key_top = jax.random.split(jax.random.fold_in(key, 12), 4)
    heavy = jax.random.randint(key_heavy, (NDEV,), 0, 8, dtype=jnp.int32) == 0
    light_load = jax.random.randint(key_light, (NDEV,), NEAR_CAP // 6, NEAR_CAP // 2 + 1, dtype=jnp.int32)
    busy_load = jax.random.randint(key_busy, (NDEV,), 3 * NEAR_CAP // 4, NEAR_CAP + 1, dtype=jnp.int32)
    loads = jnp.where(heavy, busy_load, light_load)
    fullest = jax.random.randint(key_top, (), 0, NDEV, dtype=jnp.int32)
    return jnp.where(jnp.arange(NDEV, dtype=jnp.int32) == fullest, NEAR_CAP, loads).astype(jnp.int32)


def draw_low_pairs(key, part):
    key_target, key_side, key_source = jax.random.split(jax.random.fold_in(key, 13), 3)
    total_slots = NDEV * LOW_DEV
    tree_depth = LEAVES_DEV.bit_length() - 1
    slot_dev = jnp.arange(total_slots, dtype=jnp.int32) // LOW_DEV
    local_id = jax.random.randint(key_target, (total_slots,), 0, LOWCL, dtype=jnp.int32)
    level_of = jnp.zeros((total_slots,), jnp.int32)
    for height in range(1, tree_depth):
        level_of = level_of + (local_id >= 2 * LEAVES_DEV - 2 * (LEAVES_DEV >> height)).astype(jnp.int32)
    breadth = jnp.right_shift(jnp.full((total_slots,), LEAVES_DEV, jnp.int32), level_of)
    level_start = 2 * LEAVES_DEV - 2 * breadth
    side_dev = jnp.clip(slot_dev + jax.random.randint(key_side, (total_slots,), -1, 2, dtype=jnp.int32), 0, NDEV - 1)
    source_local = level_start + jax.random.randint(key_source, (total_slots,), 0, breadth, dtype=jnp.int32)
    return jnp.stack([slot_dev * LOWCL + local_id, side_dev * LOWCL + source_local])


def draw_upper_pairs(key, part):
    key_target, key_source = jax.random.split(jax.random.fold_in(key, 14))
    total_slots = NDEV * UP_DEV
    upper_depth = NDEV.bit_length() - 1
    target = jax.random.randint(key_target, (total_slots,), 0, 2 * NDEV - 2, dtype=jnp.int32)
    level_of = jnp.zeros((total_slots,), jnp.int32)
    for height in range(1, upper_depth):
        level_of = level_of + (target >= 2 * NDEV - 2 * (NDEV >> height)).astype(jnp.int32)
    breadth = jnp.right_shift(jnp.full((total_slots,), NDEV, jnp.int32), level_of)
    level_start = 2 * NDEV - 2 * breadth
    shift_by = jax.random.randint(key_source, (total_slots,), 1, breadth, dtype=jnp.int32)
    source = level_start + (target - level_start + shift_by) % breadth
    return jnp.stack([target, source])


def steps_of(own_key, extent, cuts, least, high):
    factor_of, own = 1.0, jax.random.fold_in(own_key, 6)
    for position, blocks in cuts:
        heights = jnp.exp(jax.random.uniform(jax.random.fold_in(own, position), (blocks,), jnp.float32, least / len(cuts), high / len(cuts)))
        factor_of = factor_of * jnp.repeat(heights, extent[position] // blocks).reshape([-1 if axis == position else 1 for axis in range(len(extent))])
    return factor_of


def bell_draw(own_key, dims, scale, bound, shards=(), kind=jnp.bfloat16):
    values = scale * jax.random.normal(own_key, dims, jnp.float32)
    if shards:
        values = values * steps_of(own_key, dims, shards, -0.22, 0.18)
    return jnp.clip(values, -bound, bound).astype(kind)


def setup_inputs(seed: int = 0) -> dict:
    keys = jax.random.split(jax.random.key(seed), 12)
    coords = draw_coords(jax.random.fold_in(keys[11], 71), 0)
    rhs = bell_draw(keys[1], (NVEC, NPTS), 1.0, 6.0, ((1, 256),))
    leaf_basis = bell_draw(keys[2], (RANK, NPTS), LEAF ** -0.5, 0.375, ((1, 256),))
    low_transfer = bell_draw(keys[3], (NDEV * LOWCL, RANK, RANK), (2 * RANK) ** -0.5, 0.5, ((0, 256),))
    low_pairs = draw_low_pairs(jax.random.fold_in(keys[11], 71), 0)
    low_blocks = bell_draw(keys[5], (NDEV * LOW_DEV, RANK, RANK), RANK ** -0.5, 0.75, ((0, 256),))
    upper_transfer = bell_draw(keys[6], (2 * NDEV - 2, RANK, RANK), (2 * RANK) ** -0.5, 0.5)
    upper_pairs = draw_upper_pairs(jax.random.fold_in(keys[11], 71), 0)
    upper_blocks = bell_draw(keys[8], (NDEV * UP_DEV, RANK, RANK), RANK ** -0.5, 0.75, ((0, 256),))
    near_pairs = draw_near_pairs(jax.random.fold_in(keys[11], 71), 0)
    near_count = draw_near_count(jax.random.fold_in(keys[11], 71), 0)
    return dict(coords=coords, rhs=rhs, leaf_basis=leaf_basis, low_transfer=low_transfer, low_pairs=low_pairs, low_blocks=low_blocks, upper_transfer=upper_transfer, upper_pairs=upper_pairs, upper_blocks=upper_blocks, near_pairs=near_pairs, near_count=near_count)


amplitude = 0.0625
steepness = 1.7320508075688772
block_pairs = 32
highest = lax.Precision.HIGHEST

def matern(target_xyz, source_xyz):
    diff_x = target_xyz[0][:, :, None] - source_xyz[0][:, None, :]
    diff_y = target_xyz[1][:, :, None] - source_xyz[1][:, None, :]
    diff_z = target_xyz[2][:, :, None] - source_xyz[2][:, None, :]
    scaled = steepness * jnp.sqrt(diff_x * diff_x + diff_y * diff_y + diff_z * diff_z)
    return (amplitude * (1.0 + scaled) * jnp.exp(-scaled)).astype(jnp.bfloat16)

def reference(coords, rhs, leaf_basis, low_transfer, low_pairs, low_blocks, upper_transfer, upper_pairs, upper_blocks, near_pairs, near_count):
    tree_depth = LEAVES_DEV.bit_length() - 1
    upper_depth = NDEV.bit_length() - 1
    basis_grid = leaf_basis.astype(jnp.float32).reshape(RANK, NDEV, LEAVES_DEV, LEAF)
    rhs_grid = rhs.astype(jnp.float32).reshape(NVEC, NDEV, LEAVES_DEV, LEAF)
    current = jnp.einsum('rdlp,vdlp->dlrv', basis_grid, rhs_grid)
    transfer_grid = low_transfer.astype(jnp.float32).reshape(NDEV, LOWCL, RANK, RANK)
    tables = [current]
    start_at = 0
    breadth = LEAVES_DEV
    for height in range(tree_depth):
        lifted = jnp.einsum('dnrs,dnrv->dnsv', transfer_grid[:, start_at:start_at + breadth], current, precision=highest)
        current = lifted[:, 0::2] + lifted[:, 1::2]
        tables.append(current)
        start_at += breadth
        breadth //= 2
    low_table = jnp.concatenate(tables[:-1], axis=1)
    roots = current[:, 0]
    upper_grid = upper_transfer.astype(jnp.float32)
    upper_levels = [roots]
    current = roots
    start_at = 0
    breadth = NDEV
    for height in range(upper_depth):
        lifted = jnp.einsum('nrs,nrv->nsv', upper_grid[start_at:start_at + breadth], current, precision=highest)
        current = lifted[0::2] + lifted[1::2]
        upper_levels.append(current)
        start_at += breadth
        breadth //= 2
    upper_levels.append(jnp.zeros((1, RANK, NVEC), jnp.float32))
    upper_table = jnp.concatenate(upper_levels, axis=0)
    coupled_up = jnp.einsum('kab,kbv->kav', upper_blocks.astype(jnp.float32), upper_table[upper_pairs[1]], precision=highest)
    summed_up = jax.ops.segment_sum(coupled_up, upper_pairs[0], num_segments=2 * NDEV)
    current = summed_up[2 * NDEV - 2:2 * NDEV - 1]
    for height in reversed(range(upper_depth)):
        breadth = NDEV >> height
        start_at = 2 * NDEV - 2 * breadth
        spread = jnp.repeat(current, 2, axis=0)
        current = summed_up[start_at:start_at + breadth] + jnp.einsum('nrs,nsv->nrv', upper_grid[start_at:start_at + breadth], spread, precision=highest)
    low_flat = low_table.reshape(NDEV * LOWCL, RANK, NVEC)
    coupled_low = jnp.einsum('kab,kbv->kav', low_blocks.astype(jnp.float32), low_flat[low_pairs[1]], precision=highest)
    summed_low = jax.ops.segment_sum(coupled_low, low_pairs[0], num_segments=NDEV * LOWCL).reshape(NDEV, LOWCL, RANK, NVEC)
    current = current[:, None]
    for height in reversed(range(tree_depth)):
        breadth = LEAVES_DEV >> height
        start_at = 2 * LEAVES_DEV - 2 * breadth
        spread = jnp.repeat(current, 2, axis=1)
        current = summed_low[:, start_at:start_at + breadth] + jnp.einsum('dnrs,dnsv->dnrv', transfer_grid[:, start_at:start_at + breadth], spread, precision=highest)
    leaf_down = current.astype(jnp.bfloat16)
    far_field = jnp.einsum('dlrv,rdlp->vdlp', leaf_down.astype(jnp.float32), basis_grid)
    places = coords.astype(jnp.float32).reshape(3, NLEAVES, LEAF)
    leaf_rhs = rhs.reshape(NVEC, NLEAVES, LEAF)
    pair_grid = jnp.transpose(near_pairs.reshape(2, NDEV, NEAR_CAP), (1, 0, 2))
    block_total = (NEAR_CAP + block_pairs - 1) // block_pairs

    def one_device(packed):
        pair_block, live_pairs, device = packed

        def accumulate(block_idx, running):
            slot_ids = block_idx * block_pairs + jnp.arange(block_pairs, dtype=jnp.int32)
            live_mask = (slot_ids < live_pairs).astype(running.dtype)
            clipped = jnp.minimum(slot_ids, NEAR_CAP - 1)
            targets = pair_block[0, clipped]
            sources = pair_block[1, clipped]
            kernel = matern(places[:, targets], places[:, sources]).astype(jnp.float32)
            increment = jnp.einsum('vps,pts->vpt', leaf_rhs[:, sources].astype(jnp.float32), kernel)
            return running.at[:, targets - device * LEAVES_DEV, :].add(increment * live_mask[None, :, None])
        blank_sum = jnp.zeros((NVEC, LEAVES_DEV, LEAF), jnp.float32)
        return lax.fori_loop(0, block_total, accumulate, blank_sum)
    near_grid = lax.map(one_device, (pair_grid, near_count, jnp.arange(NDEV, dtype=jnp.int32)))
    near_flat = jnp.transpose(near_grid, (1, 0, 2, 3)).reshape(NVEC, NPTS)
    return far_field.reshape(NVEC, NPTS) + near_flat
```

```python
import jax
import jax.numpy as jnp
from jax import lax
from jax.experimental import pallas as pl
from jax.experimental.pallas import tpu as pltpu
from jax.sharding import PartitionSpec as P

LEAF = 256
MEMB = 16
ROWS = 40
C2 = 6.244106943016823
AMP = 0.0625
LN2 = 0.6931471805599453
MESH = pl.DeviceIdType.MESH
F32 = jnp.float32
BF16 = jnp.bfloat16


def dot(a, b, nt=False):
    dims = (((1,), (1,)), ((), ())) if nt else (((1,), (0,)), ((), ()))
    return lax.dot_general(a, b, dims, preferred_element_type=F32)


def split2(c):
    hi = c.astype(BF16)
    lo = (c - hi.astype(F32)).astype(BF16)
    return jnp.concatenate([hi, lo], axis=0)


def dot2(c, w, nt=False):
    n = c.shape[0]
    r = dot(split2(c), w, nt)
    return r[:n] + r[n:]


def pack(c):
    h = c.shape[0] // 2
    return jnp.concatenate([c[:h], c[h:]], axis=1)


def unpack(p):
    h = p.shape[1] // 2
    return jnp.concatenate([p[:, :h], p[:, h:]], axis=0)


def split3(x):
    a = x.astype(BF16).astype(F32)
    y = x - a
    b = y.astype(BF16).astype(F32)
    return a, b, (y - b).astype(BF16).astype(F32)


def features(xyz):
    x, y, z = xyz[0:1], xyz[1:2], xyz[2:3]
    norm = C2 * (x * x + y * y + z * z)
    n = split3(norm)
    m = [split3(-2.0 * C2 * v) for v in (x, y, z)]
    one = jnp.ones_like(x)
    zero = jnp.zeros_like(x)
    tgt = [x, y, z] * 3 + list(n) + [one] * 3 + [zero]
    src = [m[c][part] for part in range(3) for c in range(3)] + [one] * 3 + list(n) + [zero]
    row = lax.broadcasted_iota(jnp.int32, (16, xyz.shape[1]), 0)

    def build(rows):
        out = jnp.zeros((16, xyz.shape[1]), F32)
        for i, v in enumerate(rows[:15]):
            out = jnp.where(row == i, v, out)
        return out.astype(BF16)

    return build(tgt), build(src)


def up_levels(leaves, values, weights):
    out = list(values)
    start, breadth = 0, leaves
    while breadth > 1:
        for i in range(breadth // 2):
            left, right = start + 2 * i, start + 2 * i + 1
            out.append(dot2(out[left], weights(left)) + dot2(out[right], weights(right)))
        start += breadth
        breadth //= 2
    return out


def far_kernel(
    groups,
    coords_ref,
    rhs_ref,
    basis_ref,
    lt_ref,
    pairs_ref,
    ub_ref,
    ut_ref,
    rootd_ref,
    lowwin_ref,
    ft_ref,
    fswin_ref,
    rhswin_ref,
    eg_ref,
    req_ref,
    tab_ref,
    send2_ref,
    recv2_ref,
    s_ref,
    pr_ref,
    send3_ref,
    recv3_ref,
    tabd_ref,
    send4_ref,
    recv4_ref,
    oh3_ref,
    eg_sem,
    halo_s,
    halo_r,
    req_s,
    req_r,
    p1_s,
    p1_r,
    p2_s,
    p2_r,
    p3_s,
    p3_r,
    p4_s,
    p4_r,
):
    ndev = groups * MEMB
    subs = lax.axis_size("sub")
    per_row = subs // MEMB
    yy = lax.axis_index("grp")
    sub = lax.axis_index("sub")
    dev = yy * subs + sub
    g = dev // MEMB
    m = dev % MEMB

    def at_dev(d):
        return (d // subs, d % subs)

    def other_group(i):
        return (g + i) % groups

    def other_member(i):
        return (m + i) % MEMB

    barrier = pltpu.get_barrier_semaphore()

    def greet_group(i, c):
        pl.semaphore_signal(barrier, inc=1, device_id=at_dev(other_group(i) * MEMB + m), device_id_type=MESH)
        return c

    def greet_member(i, c):
        pl.semaphore_signal(barrier, inc=1, device_id=at_dev(g * MEMB + other_member(i)), device_id_type=MESH)
        return c

    after, before = (dev + 1) % ndev, (dev + ndev - 1) % ndev
    lax.fori_loop(1, groups, greet_group, 0)
    lax.fori_loop(1, MEMB, greet_member, 0)
    for d in (after, before):
        pl.semaphore_signal(barrier, inc=1, device_id=at_dev(d), device_id_type=MESH)

    depth = ndev.bit_length() - 1
    copies = []
    row = 0
    for level in range(min(7, depth - 1)):
        base = 2 * ndev - 2 * (ndev >> level)
        count = max(1, MEMB >> level)
        at = base + (g * count if level <= 4 else g // (1 << (level - 4)))
        copies.append(
            pltpu.make_async_copy(ut_ref.at[pl.ds(at, count)], eg_ref.at[pl.ds(row, count)], eg_sem.at[level])
        )
        copies[-1].start()
        row += count

    srow = lax.broadcasted_iota(jnp.int32, (8, 128), 0)
    slane = lax.broadcasted_iota(jnp.int32, (8, 128), 1)
    tile = jnp.zeros((8, 128), jnp.int32)
    for i in range(8):
        tile = jnp.where(srow == i, jnp.where(slane < 64, pairs_ref[1, i], pairs_ref[0, i]), tile)
    req_ref[g] = tile

    leaves = rhs_ref.shape[1] // LEAF
    first = [
        dot(rhs_ref[:, l * LEAF : (l + 1) * LEAF], basis_ref[:, l * LEAF : (l + 1) * LEAF], nt=True)
        for l in range(leaves)
    ]
    low = up_levels(leaves, first, lambda i: lt_ref[i])
    for i in range(2 * leaves - 2):
        lowwin_ref[1, i] = low[i]
    tab_ref[MEMB * 16 :, :] = jnp.zeros(((ROWS - MEMB) * 16, 128), F32)
    mine = pl.ds(pl.multiple_of(m * 16, 16), 16)
    tab_ref[mine, :] = pack(low[-1])
    ft, fs = features(coords_ref[...].astype(F32))
    ft_ref[...] = ft
    fswin_ref[1] = fs
    rhswin_ref[1] = rhs_ref[...]

    pl.semaphore_wait(barrier, groups - 1 + MEMB - 1 + 2)

    def copy1(i):
        return pltpu.make_async_remote_copy(
            tab_ref.at[mine], tab_ref.at[mine], p1_s.at[i], p1_r.at[i],
            device_id=at_dev(g * MEMB + other_member(i)), device_id_type=MESH)

    def copy_req(i):
        return pltpu.make_async_remote_copy(
            req_ref.at[g], req_ref.at[g], req_s.at[i], req_r.at[i],
            device_id=at_dev(other_group(i) * MEMB + m), device_id_type=MESH)

    def start(copy, lo, hi):
        def body(i, c):
            copy(i).start()
            return c
        lax.fori_loop(lo, hi, body, 0)

    def await_recv(copy, lo, hi):
        def body(i, c):
            copy(i).wait_recv()
            return c
        lax.fori_loop(lo, hi, body, 0)

    def await_send(copy, lo, hi):
        def body(i, c):
            copy(i).wait_send()
            return c
        lax.fori_loop(lo, hi, body, 0)

    start(copy1, 1, MEMB)
    start(copy_req, 1, groups)
    halo = []
    for side, to in ((0, after), (2, before)):
        for j, ref in enumerate((lowwin_ref, fswin_ref, rhswin_ref)):
            k = (side // 2) * 3 + j
            halo.append(
                pltpu.make_async_remote_copy(
                    ref.at[1], ref.at[side], halo_s.at[k], halo_r.at[k],
                    device_id=at_dev(to), device_id_type=MESH))
    for c in halo:
        c.start()

    lane = lax.broadcasted_iota(jnp.int32, (1, 2 * ROWS), 1)
    half = lane // ROWS
    trow = lane % ROWS
    cid = jnp.full((1, 2 * ROWS), -1, jnp.int32)
    row = 0
    for level in range(depth):
        base = 2 * ndev - 2 * (ndev >> level)
        count = max(1, MEMB >> level)
        at = base + (g * count if level <= 4 else g // (1 << (level - 4)))
        cid = jnp.where((trow >= row) & (trow < row + count), at + trow - row, cid)
        row += count

    await_recv(copy_req, 1, groups)

    def onehot(column):
        pieces = []
        for other in range(groups):
            eq = (column[other] == cid).astype(F32)
            for part in range(2):
                pieces.append(jnp.where(half == part, eq, 0.0))
        return jnp.concatenate(pieces, axis=0)

    req = req_ref[...]
    oh2 = onehot([req[o][:, 0:1] for o in range(groups)]).astype(BF16)
    oh3_ref[...] = jnp.transpose(onehot([req[o][:, 64:65] for o in range(groups)])).astype(BF16)

    for c in copies:
        c.wait()
    await_recv(copy1, 1, MEMB)

    roots = [unpack(tab_ref[i * 16 : (i + 1) * 16, :]) for i in range(MEMB)]
    table = up_levels(MEMB, roots, lambda i: eg_ref[i])
    for level in range(5, depth):
        table.append(dot2(table[-1], eg_ref[len(table) - 1]))
    for i in range(MEMB, len(table)):
        tab_ref[i * 16 : (i + 1) * 16, :] = pack(table[i])

    for vq in range(8):
        t = jnp.concatenate([tab_ref[pl.ds(vs * 8 + vq, ROWS, stride=16), :] for vs in range(2)], axis=0)
        out = dot(oh2, t.astype(BF16)).astype(BF16)
        send2_ref[:, vq * 16 : (vq + 1) * 16, :] = out.reshape(groups, 16, 128)
    recv2_ref[g] = send2_ref[g]

    def copy2(i):
        return pltpu.make_async_remote_copy(
            send2_ref.at[other_group(i)], recv2_ref.at[g], p2_s.at[i], p2_r.at[i],
            device_id=at_dev(other_group(i) * MEMB + m), device_id_type=MESH)

    start(copy2, 1, groups)
    await_recv(copy2, 1, groups)
    total = recv2_ref[0].astype(F32)
    for o in range(1, groups):
        total = total + recv2_ref[o].astype(F32)
    s_ref[...] = total

    for i in range(8):
        x = jnp.concatenate([s_ref[pl.ds(vs * 8 + i, 8, stride=16), :] for vs in range(2)], axis=0)
        pr_ref[i * 16 : (i + 1) * 16, :] = pack(dot2(unpack(x), ub_ref[i], nt=True))
    send3_ref[...] = jnp.concatenate(
        [pr_ref[pl.ds(vs * 8 + vq, 8, stride=16), :] for vq in range(8) for vs in range(2)], axis=0
    ).astype(BF16)
    recv3_ref[g] = send3_ref[...]

    def copy3(i):
        return pltpu.make_async_remote_copy(
            send3_ref, recv3_ref.at[g], p3_s.at[i], p3_r.at[i],
            device_id=at_dev(other_group(i) * MEMB + m), device_id_type=MESH)

    start(copy3, 1, groups)
    await_recv(copy3, 1, groups)

    oh3 = oh3_ref[...]
    for vq in range(8):
        r = recv3_ref[:, vq * 16 : (vq + 1) * 16, :].reshape(groups * 16, 128)
        tabd_ref[vq * 2 * ROWS : (vq + 1) * 2 * ROWS, :] = dot(oh3, r)

    def summed(c):
        return unpack(
            jnp.concatenate([tabd_ref[pl.ds(vs * ROWS + c, 8, stride=2 * ROWS), :] for vs in range(2)], axis=0)
        )

    at = len(table) - 1
    down = summed(at)
    while at > 2 * MEMB - 2:
        at -= 1
        down = summed(at) + dot2(down, eg_ref[at], nt=True)
    current = [down]
    breadth = 2
    while breadth <= MEMB:
        at = 2 * MEMB - 2 * breadth
        current = [summed(at + i) + dot2(current[i // 2], eg_ref[at + i], nt=True) for i in range(breadth)]
        breadth *= 2
    for i in range(MEMB):
        send4_ref[i] = pack(current[i])
    recv4_ref[m] = send4_ref[m]

    def copy4(i):
        return pltpu.make_async_remote_copy(
            send4_ref.at[other_member(i)], recv4_ref.at[m], p4_s.at[i], p4_r.at[i],
            device_id=at_dev(g * MEMB + other_member(i)), device_id_type=MESH)

    start(copy4, 1, MEMB)
    await_recv(copy4, 1, MEMB)
    total = recv4_ref[0]
    for i in range(1, MEMB):
        total = total + recv4_ref[i]
    rootd_ref[...] = total

    for c in halo:
        c.wait()
    await_send(copy_req, 1, groups)
    await_send(copy1, 1, MEMB)
    await_send(copy2, 1, groups)
    await_send(copy3, 1, groups)
    await_send(copy4, 1, MEMB)


def near_kernel(
    np_ref,
    nc_ref,
    lp_ref,
    ft_ref,
    fswin_ref,
    rhswin_ref,
    basis_ref,
    lt_ref,
    lb_ref,
    lowwin_ref,
    rootd_ref,
    out_ref,
    fst_ref,
    rw_ref,
    ftl_ref,
    acc_ref,
    lowacc_ref,
):
    dev = lax.axis_index("grp") * lax.axis_size("sub") + lax.axis_index("sub")
    leaves = out_ref.shape[1] // LEAF
    low_count = 2 * leaves - 2
    for i in range(low_count):
        lowacc_ref[i] = jnp.zeros(lowacc_ref.shape[1:], F32)
    for k in range(lp_ref.shape[1]):
        s = lp_ref[1, k] - (dev - 1) * low_count
        t = lp_ref[0, k] - dev * low_count
        prod = dot2(lowwin_ref[s // low_count, s % low_count], lb_ref[k], nt=True)
        lowacc_ref[t] = lowacc_ref[t] + prod
    current = [unpack(rootd_ref[...])]
    breadth = 2
    while breadth <= leaves:
        at = 2 * leaves - 2 * breadth
        current = [lowacc_ref[at + i] + dot2(current[i // 2], lt_ref[at + i], nt=True) for i in range(breadth)]
        breadth *= 2
    for l in range(leaves):
        acc_ref[l] = dot2(current[l], basis_ref[:, l * LEAF : (l + 1) * LEAF])
    for w in range(3):
        for l in range(leaves):
            cols = slice(l * LEAF, (l + 1) * LEAF)
            fst_ref[w * leaves + l] = jnp.transpose(fswin_ref[w, :, cols].astype(F32)).astype(BF16)
            rw_ref[w * leaves + l] = rhswin_ref[w, :, cols]
    for l in range(leaves):
        ftl_ref[l] = ft_ref[:, l * LEAF : (l + 1) * LEAF]

    def body(k, c):
        t = np_ref[0, k] - dev * leaves
        s = np_ref[1, k] - (dev - 1) * leaves
        sq = jnp.maximum(dot(fst_ref[s], ftl_ref[t]), 1e-30)
        p = sq * lax.rsqrt(sq)
        tile = ((AMP + (AMP * LN2) * p) * jnp.exp2(-p)).astype(BF16)
        acc_ref[t] = acc_ref[t] + dot(rw_ref[s], tile)
        return c

    lax.fori_loop(0, nc_ref[0], body, 0)
    for l in range(leaves):
        out_ref[:, l * LEAF : (l + 1) * LEAF] = acc_ref[l]


def on_device(coords, rhs, basis, lt, lp, lb, ut, up, ub, npairs, ncount):
    ndev = lax.axis_size(("grp", "sub"))
    groups = ndev // MEMB
    points = rhs.shape[1]
    leaves = points // LEAF
    low_count = 2 * leaves - 2
    vm = pl.BlockSpec(memory_space=pltpu.VMEM)
    sm = pl.BlockSpec(memory_space=pltpu.SMEM)
    dma = pltpu.SemaphoreType.DMA
    rootd, lowwin, ft, fswin, rhswin = pl.pallas_call(
        lambda *refs: far_kernel(groups, *refs),
        out_shape=[
            jax.ShapeDtypeStruct((16, 128), F32),
            jax.ShapeDtypeStruct((3, low_count, 32, 64), F32),
            jax.ShapeDtypeStruct((16, points), BF16),
            jax.ShapeDtypeStruct((3, 16, points), BF16),
            jax.ShapeDtypeStruct((3, 32, points), BF16),
        ],
        in_specs=[vm, vm, vm, vm, sm, vm, pl.BlockSpec(memory_space=pl.ANY)],
        out_specs=[vm] * 5,
        scratch_shapes=[
            pltpu.VMEM((ROWS, 64, 64), BF16),
            pltpu.VMEM((groups, 8, 128), jnp.int32),
            pltpu.VMEM((ROWS * 16, 128), F32),
            pltpu.VMEM((groups, 128, 128), BF16),
            pltpu.VMEM((groups, 128, 128), BF16),
            pltpu.VMEM((128, 128), F32),
            pltpu.VMEM((128, 128), F32),
            pltpu.VMEM((128, 128), BF16),
            pltpu.VMEM((groups, 128, 128), BF16),
            pltpu.VMEM((8 * 2 * ROWS, 128), F32),
            pltpu.VMEM((MEMB, 16, 128), F32),
            pltpu.VMEM((MEMB, 16, 128), F32),
            pltpu.VMEM((2 * ROWS, groups * 16), BF16),
            dma((8,)),
            dma((6,)),
            dma((6,)),
            dma((groups,)),
            dma((groups,)),
            dma((MEMB,)),
            dma((MEMB,)),
            dma((groups,)),
            dma((groups,)),
            dma((groups,)),
            dma((groups,)),
            dma((MEMB,)),
            dma((MEMB,)),
        ],
        compiler_params=pltpu.CompilerParams(
            collective_id=0, has_side_effects=True, vmem_limit_bytes=40 * 2**20
        ),
        name="far_exchange",
    )(coords, rhs, basis, lt, up, ub, ut)
    return pl.pallas_call(
        near_kernel,
        out_shape=jax.ShapeDtypeStruct((32, points), F32),
        in_specs=[sm, sm, sm] + [vm] * 8,
        out_specs=vm,
        scratch_shapes=[
            pltpu.VMEM((3 * leaves, LEAF, 16), BF16),
            pltpu.VMEM((3 * leaves, 32, LEAF), BF16),
            pltpu.VMEM((leaves, 16, LEAF), BF16),
            pltpu.VMEM((leaves, 32, LEAF), F32),
            pltpu.VMEM((low_count, 32, 64), F32),
        ],
        compiler_params=pltpu.CompilerParams(vmem_limit_bytes=40 * 2**20),
        name="near_field",
    )(npairs, ncount, lp, ft, fswin, rhswin, basis, lt, lb, lowwin, rootd)


def solution(mesh):
    both = ("grp", "sub")
    in_specs = (
        P(None, both), P(None, both), P(None, both), P(both), P(None, both), P(both),
        P(), P(None, both), P(both), P(None, both), P(both),
    )
    return jax.shard_map(on_device, mesh=mesh, in_specs=in_specs, out_specs=P(None, both), check_vma=False)
```

```python
import jax
import jax.numpy as jnp
from jax import lax
from jax.experimental import pallas as pl
from jax.experimental.pallas import tpu as pltpu
from jax.sharding import PartitionSpec as P

LEAF = 256
MEMB = 16
ROWS = 40
C2 = 6.244106943016823
AMP = 0.0625
LN2 = 0.6931471805599453
UNROLL = 4
CUT = (32, 64)
MESH = pl.DeviceIdType.MESH
F32 = jnp.float32
BF16 = jnp.bfloat16


def dot(a, b, nt=False):
    dims = (((1,), (1,)), ((), ())) if nt else (((1,), (0,)), ((), ()))
    return lax.dot_general(a, b, dims, preferred_element_type=F32)


def split2(c):
    hi = c.astype(BF16)
    lo = (c - hi.astype(F32)).astype(BF16)
    return jnp.concatenate([hi, lo], axis=0)


def dot2(c, w, nt=False):
    n = c.shape[0]
    r = dot(split2(c), w, nt)
    return r[:n] + r[n:]


def pack(c):
    h = c.shape[0] // 2
    return jnp.concatenate([c[:h], c[h:]], axis=1)


def unpack(p):
    h = p.shape[1] // 2
    return jnp.concatenate([p[:, :h], p[:, h:]], axis=0)


def split3(x):
    a = x.astype(BF16).astype(F32)
    y = x - a
    b = y.astype(BF16).astype(F32)
    return a, b, (y - b).astype(BF16).astype(F32)


def features(xyz):
    x, y, z = xyz[0:1], xyz[1:2], xyz[2:3]
    norm = C2 * (x * x + y * y + z * z)
    n = split3(norm)
    m = [split3(-2.0 * C2 * v) for v in (x, y, z)]
    one = jnp.ones_like(x)
    zero = jnp.zeros_like(x)
    tgt = [x, y, z] * 3 + list(n) + [one] * 3 + [zero]
    src = [m[c][part] for part in range(3) for c in range(3)] + [one] * 3 + list(n) + [zero]
    row = lax.broadcasted_iota(jnp.int32, (16, xyz.shape[1]), 0)

    def build(rows):
        out = jnp.zeros((16, xyz.shape[1]), F32)
        for i, v in enumerate(rows[:15]):
            out = jnp.where(row == i, v, out)
        return out.astype(BF16)

    return build(tgt), build(src)


def up_levels(leaves, values, weights):
    out = list(values)
    start, breadth = 0, leaves
    while breadth > 1:
        for i in range(breadth // 2):
            left, right = start + 2 * i, start + 2 * i + 1
            out.append(dot2(out[left], weights(left)) + dot2(out[right], weights(right)))
        start += breadth
        breadth //= 2
    return out


def kernel(
    groups,
    coords_ref,
    rhs_ref,
    basis_ref,
    lt_ref,
    lb_ref,
    upairs_ref,
    ub_ref,
    npv_ref,
    lpv_ref,
    np_ref,
    lp_ref,
    nc_ref,
    ut_ref,
    out_ref,
    utv_ref,
    ege_ref,
    eg_ref,
    meta_ref,
    smeta_ref,
    lowwin_ref,
    fswin_ref,
    rhswin_ref,
    ftl_ref,
    fst_ref,
    rw_ref,
    inc_ref,
    lowbuf_ref,
    req_ref,
    tab_ref,
    send2_ref,
    recv2_ref,
    s_ref,
    pr_ref,
    send3_ref,
    recv3_ref,
    tabd_ref,
    send4_ref,
    recv4_ref,
    oh3_ref,
    loc_sem,
    halo_s,
    halo_r,
    req_s,
    req_r,
    p1_s,
    p1_r,
    p2_s,
    p2_r,
    p3_s,
    p3_r,
    p4_s,
    p4_r,
):
    ndev = groups * MEMB
    depth = ndev.bit_length() - 1
    subs = lax.axis_size("sub")
    dev = lax.axis_index("grp") * subs + lax.axis_index("sub")
    g = dev // MEMB
    m = dev % MEMB
    leaves = rhs_ref.shape[1] // LEAF
    low_count = 2 * leaves - 2
    near_cap = npv_ref.shape[1]
    low_dev = lpv_ref.shape[1]

    def at_dev(d):
        return (d // subs, d % subs)

    def other_group(i):
        return ((g + i) % groups) * MEMB + m

    def other_member(i):
        return g * MEMB + (m + i) % MEMB

    barrier = pltpu.get_barrier_semaphore()

    def greet(to):
        def body(i, c):
            pl.semaphore_signal(barrier, inc=1, device_id=at_dev(to(i)), device_id_type=MESH)
            return c

        return body

    after, before = (dev + 1) % ndev, (dev + ndev - 1) % ndev
    lax.fori_loop(1, groups, greet(other_group), 0)
    lax.fori_loop(1, MEMB, greet(other_member), 0)
    for d in (after, before):
        pl.semaphore_signal(barrier, inc=1, device_id=at_dev(d), device_id_type=MESH)

    get_ut = pltpu.make_async_copy(ut_ref, utv_ref, loc_sem.at[0])
    get_ut.start()

    def start(copy, count):
        def body(i, c):
            copy(i).start()
            return c

        lax.fori_loop(1, count, body, 0)

    def await_recv(copy, count):
        def body(i, c):
            copy(i).wait_recv()
            return c

        lax.fori_loop(1, count, body, 0)

    def await_send(copy, count):
        def body(i, c):
            copy(i).wait_send()
            return c

        lax.fori_loop(1, count, body, 0)

    def remote(src, dst, send, recv, to):
        return pltpu.make_async_remote_copy(src, dst, send, recv, device_id=at_dev(to), device_id_type=MESH)

    srow = lax.broadcasted_iota(jnp.int32, (8, 128), 0)
    slane = lax.broadcasted_iota(jnp.int32, (8, 128), 1)
    tile = jnp.zeros((8, 128), jnp.int32)
    for i in range(8):
        tile = jnp.where(srow == i, jnp.where(slane < 64, upairs_ref[1, i], upairs_ref[0, i]), tile)
    req_ref[g] = tile

    first = [
        dot(rhs_ref[:, l * LEAF : (l + 1) * LEAF], basis_ref[:, l * LEAF : (l + 1) * LEAF], nt=True)
        for l in range(leaves)
    ]
    low = up_levels(leaves, first, lambda i: lt_ref[i])
    tab_ref[MEMB * 16 :, :] = jnp.zeros(((ROWS - MEMB) * 16, 128), F32)
    mine = pl.ds(pl.multiple_of(m * 16, 16), 16)
    tab_ref[mine, :] = pack(low[-1])
    for i in range(low_count):
        lowwin_ref[low_count + i] = pack(low[i])
    ft, fs = features(coords_ref[...].astype(F32))
    fswin_ref[1] = fs
    for l in range(leaves):
        ftl_ref[l] = ft[:, l * LEAF : (l + 1) * LEAF]

    pl.semaphore_wait(barrier, groups - 1 + MEMB - 1 + 2)

    def copy1(i):
        return remote(tab_ref.at[mine], tab_ref.at[mine], p1_s.at[i], p1_r.at[i], other_member(i))

    def copy_req(i):
        return remote(req_ref.at[g], req_ref.at[g], req_s.at[i], req_r.at[i], other_group(i))

    start(copy1, MEMB)
    start(copy_req, groups)
    halo = []
    for side, to in ((0, after), (1, before)):
        for j, (src, dst) in enumerate((
            (fswin_ref.at[1], fswin_ref.at[2 * side]),
            (rhs_ref, rhswin_ref.at[2 * side]),
            (lowwin_ref.at[pl.ds(low_count, low_count)], lowwin_ref.at[pl.ds(2 * side * low_count, low_count)]),
        )):
            k = j * 2 + side
            halo.append(remote(src, dst, halo_s.at[k], halo_r.at[k], to))
    for c in halo:
        c.start()

    def chain(pairs, live, first_target, targets):
        n = pairs.shape[1]
        t = pairs[0:1, :] - first_target
        t = jnp.concatenate([t, jnp.full((1, 128 - n), -1, jnp.int32)], axis=1)
        down = jnp.transpose(jnp.broadcast_to(t, (128, 128)))
        slot = lax.broadcasted_iota(jnp.int32, (128, 128), 0)
        lane = lax.broadcasted_iota(jnp.int32, (128, 128), 1)
        ok = slot < live
        prev = jnp.max(jnp.where(ok & (slot < lane) & (down == t), slot + 1, 0), axis=0, keepdims=True)
        last = jnp.max(jnp.where(ok & (down == lane) & (lane < targets), slot + 1, 0), axis=0, keepdims=True)
        return prev, last

    rows = chain(npv_ref[...], nc_ref[0], dev * leaves, leaves) + chain(lpv_ref[...], low_dev, dev * low_count, low_count)
    meta_ref[...] = jnp.concatenate(list(rows) + [jnp.zeros((4, 128), jnp.int32)], axis=0)
    to_scalar = pltpu.make_async_copy(meta_ref, smeta_ref, loc_sem.at[1])
    to_scalar.start()

    def row_ids(trow):
        ids = jnp.full(trow.shape, -1, jnp.int32)
        row = 0
        for level in range(depth):
            base = 2 * ndev - 2 * (ndev >> level)
            count = max(1, MEMB >> level)
            at = base + (g * count if level <= 4 else g // (1 << (level - 4)))
            ids = jnp.where((trow >= row) & (trow < row + count), at + trow - row, ids)
            row += count
        return ids

    clusters = ut_ref.shape[2]
    pick = lax.broadcasted_iota(jnp.int32, (ROWS, clusters), 1) == row_ids(
        lax.broadcasted_iota(jnp.int32, (ROWS, clusters), 0)
    )
    pick = jnp.where(pick, 1.0, 0.0).astype(BF16)
    get_ut.wait()
    for i in range(32):
        x = jnp.concatenate([utv_ref[i], utv_ref[i + 32]], axis=0)
        ege_ref[i * ROWS : (i + 1) * ROWS, :] = dot(pick, x, nt=True)
    used = 2 * MEMB - 1 + depth - 5
    for c in range(used):
        eg_ref[c] = unpack(ege_ref[pl.ds(c, 32, stride=ROWS), :]).astype(BF16)

    await_recv(copy_req, groups)
    lane = lax.broadcasted_iota(jnp.int32, (1, 2 * ROWS), 1)
    half = lane // ROWS
    cid = row_ids(lane % ROWS)

    def onehot(column):
        pieces = []
        for other in range(groups):
            eq = (column[other] == cid).astype(F32)
            for part in range(2):
                pieces.append(jnp.where(half == part, eq, 0.0))
        return jnp.concatenate(pieces, axis=0)

    req = req_ref[...]
    oh2 = onehot([req[o][:, 0:1] for o in range(groups)]).astype(BF16)
    oh3_ref[...] = jnp.transpose(onehot([req[o][:, 64:65] for o in range(groups)])).astype(BF16)

    await_recv(copy1, MEMB)

    roots = [unpack(tab_ref[i * 16 : (i + 1) * 16, :]) for i in range(MEMB)]
    table = up_levels(MEMB, roots, lambda i: eg_ref[i])
    for level in range(5, depth):
        table.append(dot2(table[-1], eg_ref[len(table) - 1]))
    for i in range(MEMB, len(table)):
        tab_ref[i * 16 : (i + 1) * 16, :] = pack(table[i])

    for vq in range(8):
        t = jnp.concatenate([tab_ref[pl.ds(vs * 8 + vq, ROWS, stride=16), :] for vs in range(2)], axis=0)
        out = dot(oh2, t.astype(BF16)).astype(BF16)
        send2_ref[:, vq * 16 : (vq + 1) * 16, :] = out.reshape(groups, 16, 128)
    recv2_ref[g] = send2_ref[g]

    def copy2(i):
        return remote(send2_ref.at[(g + i) % groups], recv2_ref.at[g], p2_s.at[i], p2_r.at[i], other_group(i))

    start(copy2, groups)

    to_scalar.wait()
    for c in halo:
        c.wait_recv()
    inc_ref[0] = jnp.zeros(inc_ref.shape[1:], F32)
    for w in range(3):
        for l in range(leaves):
            cols = slice(l * LEAF, (l + 1) * LEAF)
            fst_ref[w * leaves + l] = jnp.transpose(fswin_ref[w, :, cols].astype(F32)).astype(BF16)
            rw_ref[w * leaves + l] = rhs_ref[:, cols] if w == 1 else rhswin_ref[w, :, cols]

    def near(lo, hi):
        def body(b, c):
            made = []
            for u in range(UNROLL):
                k = b * UNROLL + u
                t = jnp.clip(np_ref[0, k] - dev * leaves, 0, leaves - 1)
                s = jnp.clip(np_ref[1, k] - (dev - 1) * leaves, 0, 3 * leaves - 1)
                sq = jnp.maximum(dot(fst_ref[s], ftl_ref[t]), 1e-30)
                p = sq * lax.rsqrt(sq)
                tile = ((AMP + (AMP * LN2) * p) * jnp.exp2(-p)).astype(BF16)
                made.append(dot(rw_ref[s], tile))
            for u in range(UNROLL):
                k = b * UNROLL + u
                inc_ref[k + 1] = made[u] + inc_ref[smeta_ref[0, k]]
            return c

        lax.fori_loop(lo // UNROLL, hi // UNROLL, body, 0)

    near(0, CUT[0])
    await_recv(copy2, groups)
    total = recv2_ref[0].astype(F32)
    for o in range(1, groups):
        total = total + recv2_ref[o].astype(F32)
    s_ref[...] = total

    for i in range(8):
        x = jnp.concatenate([s_ref[pl.ds(vs * 8 + i, 8, stride=16), :] for vs in range(2)], axis=0)
        pr_ref[i * 16 : (i + 1) * 16, :] = pack(dot2(unpack(x), ub_ref[i], nt=True))
    send3_ref[...] = jnp.concatenate(
        [pr_ref[pl.ds(vs * 8 + vq, 8, stride=16), :] for vq in range(8) for vs in range(2)], axis=0
    ).astype(BF16)
    recv3_ref[g] = send3_ref[...]

    def copy3(i):
        return remote(send3_ref, recv3_ref.at[g], p3_s.at[i], p3_r.at[i], other_group(i))

    start(copy3, groups)
    near(CUT[0], CUT[1])
    await_recv(copy3, groups)

    oh3 = oh3_ref[...]
    for vq in range(8):
        r = recv3_ref[:, vq * 16 : (vq + 1) * 16, :].reshape(groups * 16, 128)
        tabd_ref[vq * 2 * ROWS : (vq + 1) * 2 * ROWS, :] = dot(oh3, r)

    def summed(c):
        return unpack(
            jnp.concatenate([tabd_ref[pl.ds(vs * ROWS + c, 8, stride=2 * ROWS), :] for vs in range(2)], axis=0)
        )

    at = len(table) - 1
    down = summed(at)
    while at > 2 * MEMB - 2:
        at -= 1
        down = summed(at) + dot2(down, eg_ref[at], nt=True)
    current = [down]
    breadth = 2
    while breadth <= MEMB:
        at = 2 * MEMB - 2 * breadth
        current = [summed(at + i) + dot2(current[i // 2], eg_ref[at + i], nt=True) for i in range(breadth)]
        breadth *= 2
    for i in range(MEMB):
        send4_ref[i] = pack(current[i])
    recv4_ref[m] = send4_ref[m]

    def copy4(i):
        return remote(send4_ref.at[(m + i) % MEMB], recv4_ref.at[m], p4_s.at[i], p4_r.at[i], other_member(i))

    start(copy4, MEMB)

    lowbuf_ref[0] = jnp.zeros(lowbuf_ref.shape[1:], F32)
    made = []
    for k in range(low_dev):
        s = jnp.clip(lp_ref[1, k] - (dev - 1) * low_count, 0, 3 * low_count - 1)
        made.append(dot2(unpack(lowwin_ref[s]), lb_ref[k], nt=True))
    for k in range(low_dev):
        lowbuf_ref[k + 1] = made[k] + lowbuf_ref[smeta_ref[2, k]]
    near(CUT[1], near_cap)

    await_recv(copy4, MEMB)
    total = recv4_ref[0]
    for i in range(1, MEMB):
        total = total + recv4_ref[i]
    current = [unpack(total)]
    breadth = 2
    while breadth <= leaves:
        at = 2 * leaves - 2 * breadth
        current = [
            lowbuf_ref[smeta_ref[3, at + i]] + dot2(current[i // 2], lt_ref[at + i], nt=True) for i in range(breadth)
        ]
        breadth *= 2
    for l in range(leaves):
        cols = slice(l * LEAF, (l + 1) * LEAF)
        out_ref[:, cols] = inc_ref[smeta_ref[1, l]] + dot2(current[l], basis_ref[:, cols])

    for c in halo:
        c.wait_send()
    await_send(copy_req, groups)
    await_send(copy1, MEMB)
    await_send(copy2, groups)
    await_send(copy3, groups)
    await_send(copy4, MEMB)


def on_device(coords, rhs, basis, lt, lp, lb, ut, up, ub, npairs, ncount):
    ndev = lax.axis_size(("grp", "sub"))
    groups = ndev // MEMB
    points = rhs.shape[1]
    leaves = points // LEAF
    low_count = 2 * leaves - 2
    near_cap = npairs.shape[1]
    vm = pl.BlockSpec(memory_space=pltpu.VMEM)
    sm = pl.BlockSpec(memory_space=pltpu.SMEM)
    dma = pltpu.SemaphoreType.DMA
    ut = jnp.transpose(ut, (1, 2, 0))
    return pl.pallas_call(
        lambda *refs: kernel(groups, *refs),
        out_shape=jax.ShapeDtypeStruct((32, points), F32),
        in_specs=[vm, vm, vm, vm, vm, sm, vm, vm, vm, sm, sm, sm, pl.BlockSpec(memory_space=pl.ANY)],
        out_specs=vm,
        scratch_shapes=[
            pltpu.VMEM(ut.shape, BF16),
            pltpu.VMEM((32 * ROWS, 128), F32),
            pltpu.VMEM((ROWS, 64, 64), BF16),
            pltpu.VMEM((8, 128), jnp.int32),
            pltpu.SMEM((8, 128), jnp.int32),
            pltpu.VMEM((3 * low_count, 16, 128), F32),
            pltpu.VMEM((3, 16, points), BF16),
            pltpu.VMEM((3, 32, points), BF16),
            pltpu.VMEM((leaves, 16, LEAF), BF16),
            pltpu.VMEM((3 * leaves, LEAF, 16), BF16),
            pltpu.VMEM((3 * leaves, 32, LEAF), BF16),
            pltpu.VMEM((near_cap + 1, 32, LEAF), F32),
            pltpu.VMEM((lp.shape[1] + 1, 32, 64), F32),
            pltpu.VMEM((groups, 8, 128), jnp.int32),
            pltpu.VMEM((ROWS * 16, 128), F32),
            pltpu.VMEM((groups, 128, 128), BF16),
            pltpu.VMEM((groups, 128, 128), BF16),
            pltpu.VMEM((128, 128), F32),
            pltpu.VMEM((128, 128), F32),
            pltpu.VMEM((128, 128), BF16),
            pltpu.VMEM((groups, 128, 128), BF16),
            pltpu.VMEM((8 * 2 * ROWS, 128), F32),
            pltpu.VMEM((MEMB, 16, 128), F32),
            pltpu.VMEM((MEMB, 16, 128), F32),
            pltpu.VMEM((2 * ROWS, groups * 16), BF16),
            dma((2,)),
            dma((6,)),
            dma((6,)),
            dma((groups,)),
            dma((groups,)),
            dma((MEMB,)),
            dma((MEMB,)),
            dma((groups,)),
            dma((groups,)),
            dma((groups,)),
            dma((groups,)),
            dma((MEMB,)),
            dma((MEMB,)),
        ],
        compiler_params=pltpu.CompilerParams(
            collective_id=0, has_side_effects=True, vmem_limit_bytes=56 * 2**20
        ),
        name="tree_product",
    )(coords, rhs, basis, lt, lb, up, ub, npairs, lp, npairs, lp, ncount, ut)


def solution(mesh):
    both = ("grp", "sub")
    in_specs = (
        P(None, both), P(None, both), P(None, both), P(both), P(None, both), P(both),
        P(), P(None, both), P(both), P(None, both), P(both),
    )
    return jax.shard_map(on_device, mesh=mesh, in_specs=in_specs, out_specs=P(None, both), check_vma=False)
```

```python
import jax
import jax.numpy as jnp
from jax import lax
from jax.experimental import pallas as pl
from jax.experimental.pallas import tpu as pltpu
from jax.sharding import PartitionSpec as P

LEAF = 256
MEMB = 16
ROWS = 40
C2 = 6.244106943016823
AMP = 0.0625
LN2 = 0.6931471805599453
UNROLL = 4
CUT = (24, 60)
MESH = pl.DeviceIdType.MESH
F32 = jnp.float32
BF16 = jnp.bfloat16


def dot(a, b, nt=False):
    dims = (((1,), (1,)), ((), ())) if nt else (((1,), (0,)), ((), ()))
    return lax.dot_general(a, b, dims, preferred_element_type=F32)


def split2(c):
    hi = c.astype(BF16)
    lo = (c - hi.astype(F32)).astype(BF16)
    return jnp.concatenate([hi, lo], axis=0)


def dot2(c, w, nt=False):
    n = c.shape[0]
    r = dot(split2(c), w, nt)
    return r[:n] + r[n:]


def pack(c):
    h = c.shape[0] // 2
    return jnp.concatenate([c[:h], c[h:]], axis=1)


def unpack(p):
    h = p.shape[1] // 2
    return jnp.concatenate([p[:, :h], p[:, h:]], axis=0)


def split3(x):
    a = x.astype(BF16).astype(F32)
    y = x - a
    b = y.astype(BF16).astype(F32)
    return a, b, (y - b).astype(BF16).astype(F32)


def features(xyz):
    x, y, z = xyz[0:1], xyz[1:2], xyz[2:3]
    norm = C2 * (x * x + y * y + z * z)
    n = split3(norm)
    m = [split3(-2.0 * C2 * v) for v in (x, y, z)]
    one = jnp.ones_like(x)
    zero = jnp.zeros_like(x)
    tgt = [x, y, z] * 3 + list(n) + [one] * 3 + [zero]
    src = [m[c][part] for part in range(3) for c in range(3)] + [one] * 3 + list(n) + [zero]
    row = lax.broadcasted_iota(jnp.int32, (16, xyz.shape[1]), 0)

    def build(rows):
        out = jnp.zeros((16, xyz.shape[1]), F32)
        for i, v in enumerate(rows[:15]):
            out = jnp.where(row == i, v, out)
        return out.astype(BF16)

    return build(tgt), build(src)


def up_levels(leaves, values, weights):
    out = list(values)
    start, breadth = 0, leaves
    while breadth > 1:
        for i in range(breadth // 2):
            left, right = start + 2 * i, start + 2 * i + 1
            out.append(dot2(out[left], weights(left)) + dot2(out[right], weights(right)))
        start += breadth
        breadth //= 2
    return out


def kernel(
    groups,
    coords_ref,
    rhs_ref,
    basis_ref,
    lt_ref,
    lbh_ref,
    upairs_ref,
    ubh_ref,
    npv_ref,
    lpv_ref,
    np_ref,
    lp_ref,
    nc_ref,
    ut_ref,
    out_ref,
    utv_ref,
    lb_ref,
    ub_ref,
    ege_ref,
    eg_ref,
    meta_ref,
    smeta_ref,
    lowwin_ref,
    fswin_ref,
    rhswin_ref,
    ftl_ref,
    fst_ref,
    rw_ref,
    inc_ref,
    lowbuf_ref,
    req_ref,
    tab_ref,
    send2_ref,
    recv2_ref,
    s_ref,
    pr_ref,
    send3_ref,
    recv3_ref,
    tabd_ref,
    send4_ref,
    recv4_ref,
    oh3_ref,
    loc_sem,
    halo_s,
    halo_r,
    req_s,
    req_r,
    p1_s,
    p1_r,
    p2_s,
    p2_r,
    p3_s,
    p3_r,
    p4_s,
    p4_r,
):
    ndev = groups * MEMB
    depth = ndev.bit_length() - 1
    subs = lax.axis_size("sub")
    dev = lax.axis_index("grp") * subs + lax.axis_index("sub")
    g = dev // MEMB
    m = dev % MEMB
    leaves = rhs_ref.shape[1] // LEAF
    low_count = 2 * leaves - 2
    near_cap = npv_ref.shape[1]
    low_dev = lpv_ref.shape[1]

    def at_dev(d):
        return (d // subs, d % subs)

    def other_group(i):
        return ((g + i) % groups) * MEMB + m

    def other_member(i):
        return g * MEMB + (m + i) % MEMB

    barrier = pltpu.get_barrier_semaphore()

    def greet(to):
        def body(i, c):
            pl.semaphore_signal(barrier, inc=1, device_id=at_dev(to(i)), device_id_type=MESH)
            return c

        return body

    after, before = (dev + 1) % ndev, (dev + ndev - 1) % ndev
    lax.fori_loop(1, groups, greet(other_group), 0)
    lax.fori_loop(1, MEMB, greet(other_member), 0)
    for d in (after, before):
        pl.semaphore_signal(barrier, inc=1, device_id=at_dev(d), device_id_type=MESH)

    get_ut = pltpu.make_async_copy(ut_ref, utv_ref, loc_sem.at[0])
    get_ub = pltpu.make_async_copy(ubh_ref, ub_ref, loc_sem.at[2])
    get_lb = pltpu.make_async_copy(lbh_ref, lb_ref, loc_sem.at[3])
    get_ut.start()
    get_ub.start()
    get_lb.start()

    def start(copy, count):
        def body(i, c):
            copy(i).start()
            return c

        lax.fori_loop(1, count, body, 0)

    def await_recv(copy, count):
        def body(i, c):
            copy(i).wait_recv()
            return c

        lax.fori_loop(1, count, body, 0)

    def await_send(copy, count):
        def body(i, c):
            copy(i).wait_send()
            return c

        lax.fori_loop(1, count, body, 0)

    def remote(src, dst, send, recv, to):
        return pltpu.make_async_remote_copy(src, dst, send, recv, device_id=at_dev(to), device_id_type=MESH)

    srow = lax.broadcasted_iota(jnp.int32, (8, 128), 0)
    slane = lax.broadcasted_iota(jnp.int32, (8, 128), 1)
    tile = jnp.zeros((8, 128), jnp.int32)
    for i in range(8):
        tile = jnp.where(srow == i, jnp.where(slane < 64, upairs_ref[1, i], upairs_ref[0, i]), tile)
    req_ref[g] = tile

    first = [
        dot(rhs_ref[:, l * LEAF : (l + 1) * LEAF], basis_ref[:, l * LEAF : (l + 1) * LEAF], nt=True)
        for l in range(leaves)
    ]
    low = up_levels(leaves, first, lambda i: lt_ref[i])
    tab_ref[MEMB * 16 :, :] = jnp.zeros(((ROWS - MEMB) * 16, 128), F32)
    mine = pl.ds(pl.multiple_of(m * 16, 16), 16)
    tab_ref[mine, :] = pack(low[-1])
    for i in range(low_count):
        lowwin_ref[low_count + i] = pack(low[i])
    ft, fs = features(coords_ref[...].astype(F32))
    fswin_ref[1] = fs
    for l in range(leaves):
        ftl_ref[l] = ft[:, l * LEAF : (l + 1) * LEAF]

    pl.semaphore_wait(barrier, groups - 1 + MEMB - 1 + 2)

    def copy1(i):
        return remote(tab_ref.at[mine], tab_ref.at[mine], p1_s.at[i], p1_r.at[i], other_member(i))

    def copy_req(i):
        return remote(req_ref.at[g], req_ref.at[g], req_s.at[i], req_r.at[i], other_group(i))

    start(copy1, MEMB)
    start(copy_req, groups)
    halo = []
    for side, to in ((0, after), (1, before)):
        for j, (src, dst) in enumerate((
            (fswin_ref.at[1], fswin_ref.at[2 * side]),
            (rhs_ref, rhswin_ref.at[2 * side]),
            (lowwin_ref.at[pl.ds(low_count, low_count)], lowwin_ref.at[pl.ds(2 * side * low_count, low_count)]),
        )):
            k = j * 2 + side
            halo.append(remote(src, dst, halo_s.at[k], halo_r.at[k], to))

    def chain(pairs, live, first_target, targets):
        n = pairs.shape[1]
        t = pairs[0:1, :] - first_target
        t = jnp.concatenate([t, jnp.full((1, 128 - n), -1, jnp.int32)], axis=1)
        down = jnp.transpose(jnp.broadcast_to(t, (128, 128)))
        slot = lax.broadcasted_iota(jnp.int32, (128, 128), 0)
        lane = lax.broadcasted_iota(jnp.int32, (128, 128), 1)
        ok = slot < live
        prev = jnp.max(jnp.where(ok & (slot < lane) & (down == t), slot + 1, 0), axis=0, keepdims=True)
        last = jnp.max(jnp.where(ok & (down == lane) & (lane < targets), slot + 1, 0), axis=0, keepdims=True)
        return prev, last

    rows = chain(npv_ref[...], nc_ref[0], dev * leaves, leaves) + chain(lpv_ref[...], low_dev, dev * low_count, low_count)
    meta_ref[...] = jnp.concatenate(list(rows) + [jnp.zeros((4, 128), jnp.int32)], axis=0)
    to_scalar = pltpu.make_async_copy(meta_ref, smeta_ref, loc_sem.at[1])
    to_scalar.start()

    def row_ids(trow):
        ids = jnp.full(trow.shape, -1, jnp.int32)
        row = 0
        for level in range(depth):
            base = 2 * ndev - 2 * (ndev >> level)
            count = max(1, MEMB >> level)
            at = base + (g * count if level <= 4 else g // (1 << (level - 4)))
            ids = jnp.where((trow >= row) & (trow < row + count), at + trow - row, ids)
            row += count
        return ids

    clusters = ut_ref.shape[2]
    pick = lax.broadcasted_iota(jnp.int32, (ROWS, clusters), 1) == row_ids(
        lax.broadcasted_iota(jnp.int32, (ROWS, clusters), 0)
    )
    pick = jnp.where(pick, 1.0, 0.0).astype(BF16)
    get_ut.wait()
    get_ub.wait()
    get_lb.wait()
    for i in range(32):
        x = jnp.concatenate([utv_ref[i], utv_ref[i + 32]], axis=0)
        ege_ref[i * ROWS : (i + 1) * ROWS, :] = dot(pick, x, nt=True)
    used = 2 * MEMB - 1 + depth - 5
    for c in range(used):
        eg_ref[c] = unpack(ege_ref[pl.ds(c, 32, stride=ROWS), :]).astype(BF16)

    await_recv(copy_req, groups)
    lane = lax.broadcasted_iota(jnp.int32, (1, 2 * ROWS), 1)
    half = lane // ROWS
    cid = row_ids(lane % ROWS)

    def onehot(column):
        pieces = []
        for other in range(groups):
            eq = (column[other] == cid).astype(F32)
            for part in range(2):
                pieces.append(jnp.where(half == part, eq, 0.0))
        return jnp.concatenate(pieces, axis=0)

    req = req_ref[...]
    oh2 = onehot([req[o][:, 0:1] for o in range(groups)]).astype(BF16)
    oh3_ref[...] = jnp.transpose(onehot([req[o][:, 64:65] for o in range(groups)])).astype(BF16)

    await_recv(copy1, MEMB)
    for c in halo:
        c.start()

    roots = [unpack(tab_ref[i * 16 : (i + 1) * 16, :]) for i in range(MEMB)]
    table = up_levels(MEMB, roots, lambda i: eg_ref[i])
    for level in range(5, depth):
        table.append(dot2(table[-1], eg_ref[len(table) - 1]))
    for i in range(MEMB, len(table)):
        tab_ref[i * 16 : (i + 1) * 16, :] = pack(table[i])

    for vq in range(8):
        t = jnp.concatenate([tab_ref[pl.ds(vs * 8 + vq, ROWS, stride=16), :] for vs in range(2)], axis=0)
        out = dot(oh2, t.astype(BF16)).astype(BF16)
        send2_ref[:, vq * 16 : (vq + 1) * 16, :] = out.reshape(groups, 16, 128)
    recv2_ref[g] = send2_ref[g]

    def copy2(i):
        return remote(send2_ref.at[(g + i) % groups], recv2_ref.at[g], p2_s.at[i], p2_r.at[i], other_group(i))

    start(copy2, groups)

    to_scalar.wait()
    for c in halo:
        c.wait_recv()
    inc_ref[0] = jnp.zeros(inc_ref.shape[1:], F32)
    for w in range(3):
        for l in range(leaves):
            cols = slice(l * LEAF, (l + 1) * LEAF)
            fst_ref[w * leaves + l] = jnp.transpose(fswin_ref[w, :, cols].astype(F32)).astype(BF16)
            rw_ref[w * leaves + l] = rhs_ref[:, cols] if w == 1 else rhswin_ref[w, :, cols]

    def near(lo, hi):
        def body(b, c):
            made = []
            for u in range(UNROLL):
                k = b * UNROLL + u
                t = jnp.clip(np_ref[0, k] - dev * leaves, 0, leaves - 1)
                s = jnp.clip(np_ref[1, k] - (dev - 1) * leaves, 0, 3 * leaves - 1)
                sq = jnp.maximum(dot(fst_ref[s], ftl_ref[t]), 1e-30)
                p = sq * lax.rsqrt(sq)
                tile = ((AMP + (AMP * LN2) * p) * jnp.exp2(-p)).astype(BF16)
                made.append(dot(rw_ref[s], tile))
            for u in range(UNROLL):
                k = b * UNROLL + u
                inc_ref[k + 1] = made[u] + inc_ref[smeta_ref[0, k]]
            return c

        lax.fori_loop(lo // UNROLL, hi // UNROLL, body, 0)

    near(0, CUT[0])
    await_recv(copy2, groups)
    total = recv2_ref[0].astype(F32)
    for o in range(1, groups):
        total = total + recv2_ref[o].astype(F32)
    s_ref[...] = total

    for i in range(8):
        x = jnp.concatenate([s_ref[pl.ds(vs * 8 + i, 8, stride=16), :] for vs in range(2)], axis=0)
        pr_ref[i * 16 : (i + 1) * 16, :] = pack(dot2(unpack(x), ub_ref[i], nt=True))
    send3_ref[...] = jnp.concatenate(
        [pr_ref[pl.ds(vs * 8 + vq, 8, stride=16), :] for vq in range(8) for vs in range(2)], axis=0
    ).astype(BF16)
    recv3_ref[g] = send3_ref[...]

    def copy3(i):
        return remote(send3_ref, recv3_ref.at[g], p3_s.at[i], p3_r.at[i], other_group(i))

    start(copy3, groups)
    near(CUT[0], CUT[1])
    await_recv(copy3, groups)

    oh3 = oh3_ref[...]
    for vq in range(8):
        r = recv3_ref[:, vq * 16 : (vq + 1) * 16, :].reshape(groups * 16, 128)
        tabd_ref[vq * 2 * ROWS : (vq + 1) * 2 * ROWS, :] = dot(oh3, r)

    def summed(c):
        return unpack(
            jnp.concatenate([tabd_ref[pl.ds(vs * ROWS + c, 8, stride=2 * ROWS), :] for vs in range(2)], axis=0)
        )

    at = len(table) - 1
    down = summed(at)
    while at > 2 * MEMB - 2:
        at -= 1
        down = summed(at) + dot2(down, eg_ref[at], nt=True)
    current = [down]
    breadth = 2
    while breadth <= MEMB:
        at = 2 * MEMB - 2 * breadth
        current = [summed(at + i) + dot2(current[i // 2], eg_ref[at + i], nt=True) for i in range(breadth)]
        breadth *= 2
    for i in range(MEMB):
        send4_ref[i] = pack(current[i])
    recv4_ref[m] = send4_ref[m]

    def copy4(i):
        return remote(send4_ref.at[(m + i) % MEMB], recv4_ref.at[m], p4_s.at[i], p4_r.at[i], other_member(i))

    start(copy4, MEMB)

    lowbuf_ref[0] = jnp.zeros(lowbuf_ref.shape[1:], F32)
    made = []
    for k in range(low_dev):
        s = jnp.clip(lp_ref[1, k] - (dev - 1) * low_count, 0, 3 * low_count - 1)
        made.append(dot2(unpack(lowwin_ref[s]), lb_ref[k], nt=True))
    for k in range(low_dev):
        lowbuf_ref[k + 1] = made[k] + lowbuf_ref[smeta_ref[2, k]]
    near(CUT[1], near_cap)

    await_recv(copy4, MEMB)
    total = recv4_ref[0]
    for i in range(1, MEMB):
        total = total + recv4_ref[i]
    current = [unpack(total)]
    breadth = 2
    while breadth <= leaves:
        at = 2 * leaves - 2 * breadth
        current = [
            lowbuf_ref[smeta_ref[3, at + i]] + dot2(current[i // 2], lt_ref[at + i], nt=True) for i in range(breadth)
        ]
        breadth *= 2
    for l in range(leaves):
        cols = slice(l * LEAF, (l + 1) * LEAF)
        out_ref[:, cols] = inc_ref[smeta_ref[1, l]] + dot2(current[l], basis_ref[:, cols])

    for c in halo:
        c.wait_send()
    await_send(copy_req, groups)
    await_send(copy1, MEMB)
    await_send(copy2, groups)
    await_send(copy3, groups)
    await_send(copy4, MEMB)


def on_device(coords, rhs, basis, lt, lp, lb, ut, up, ub, npairs, ncount):
    ndev = lax.axis_size(("grp", "sub"))
    groups = ndev // MEMB
    points = rhs.shape[1]
    leaves = points // LEAF
    low_count = 2 * leaves - 2
    near_cap = npairs.shape[1]
    vm = pl.BlockSpec(memory_space=pltpu.VMEM)
    sm = pl.BlockSpec(memory_space=pltpu.SMEM)
    anym = pl.BlockSpec(memory_space=pl.ANY)
    dma = pltpu.SemaphoreType.DMA
    ut = jnp.transpose(ut, (1, 2, 0))
    return pl.pallas_call(
        lambda *refs: kernel(groups, *refs),
        out_shape=jax.ShapeDtypeStruct((32, points), F32),
        in_specs=[vm, vm, vm, vm, anym, sm, anym, vm, vm, sm, sm, sm, anym],
        out_specs=vm,
        scratch_shapes=[
            pltpu.VMEM(ut.shape, BF16),
            pltpu.VMEM(lb.shape, BF16),
            pltpu.VMEM(ub.shape, BF16),
            pltpu.VMEM((32 * ROWS, 128), F32),
            pltpu.VMEM((ROWS, 64, 64), BF16),
            pltpu.VMEM((8, 128), jnp.int32),
            pltpu.SMEM((8, 128), jnp.int32),
            pltpu.VMEM((3 * low_count, 16, 128), F32),
            pltpu.VMEM((3, 16, points), BF16),
            pltpu.VMEM((3, 32, points), BF16),
            pltpu.VMEM((leaves, 16, LEAF), BF16),
            pltpu.VMEM((3 * leaves, LEAF, 16), BF16),
            pltpu.VMEM((3 * leaves, 32, LEAF), BF16),
            pltpu.VMEM((near_cap + 1, 32, LEAF), F32),
            pltpu.VMEM((lp.shape[1] + 1, 32, 64), F32),
            pltpu.VMEM((groups, 8, 128), jnp.int32),
            pltpu.VMEM((ROWS * 16, 128), F32),
            pltpu.VMEM((groups, 128, 128), BF16),
            pltpu.VMEM((groups, 128, 128), BF16),
            pltpu.VMEM((128, 128), F32),
            pltpu.VMEM((128, 128), F32),
            pltpu.VMEM((128, 128), BF16),
            pltpu.VMEM((groups, 128, 128), BF16),
            pltpu.VMEM((8 * 2 * ROWS, 128), F32),
            pltpu.VMEM((MEMB, 16, 128), F32),
            pltpu.VMEM((MEMB, 16, 128), F32),
            pltpu.VMEM((2 * ROWS, groups * 16), BF16),
            dma((4,)),
            dma((6,)),
            dma((6,)),
            dma((groups,)),
            dma((groups,)),
            dma((MEMB,)),
            dma((MEMB,)),
            dma((groups,)),
            dma((groups,)),
            dma((groups,)),
            dma((groups,)),
            dma((MEMB,)),
            dma((MEMB,)),
        ],
        compiler_params=pltpu.CompilerParams(
            collective_id=0, has_side_effects=True, vmem_limit_bytes=56 * 2**20
        ),
        name="tree_product",
    )(coords, rhs, basis, lt, lb, up, ub, npairs, lp, npairs, lp, ncount, ut)


def solution(mesh):
    both = ("grp", "sub")
    in_specs = (
        P(None, both), P(None, both), P(None, both), P(both), P(None, both), P(both),
        P(), P(None, both), P(both), P(None, both), P(both),
    )
    return jax.shard_map(on_device, mesh=mesh, in_specs=in_specs, out_specs=P(None, both), check_vma=False)
```

```python
import jax
import jax.numpy as jnp
from jax import lax
from jax.experimental import pallas as pl
from jax.experimental.pallas import tpu as pltpu
from jax.sharding import PartitionSpec as P

LEAF = 256
MEMB = 16
ROWS = 40
C2 = 6.244106943016823
AMP = 0.0625
LN2 = 0.6931471805599453
UNROLL = 8
CUT = (24, 24, 56, 56)
MESH = pl.DeviceIdType.MESH
F32 = jnp.float32
BF16 = jnp.bfloat16


def dot(a, b, nt=False):
    dims = (((1,), (1,)), ((), ())) if nt else (((1,), (0,)), ((), ()))
    return lax.dot_general(a, b, dims, preferred_element_type=F32)


def split2(c):
    hi = c.astype(BF16)
    lo = (c - hi.astype(F32)).astype(BF16)
    return jnp.concatenate([hi, lo], axis=0)


def dot2(c, w, nt=False):
    n = c.shape[0]
    r = dot(split2(c), w, nt)
    return r[:n] + r[n:]


def pack(c):
    h = c.shape[0] // 2
    return jnp.concatenate([c[:h], c[h:]], axis=1)


def unpack(p):
    h = p.shape[1] // 2
    return jnp.concatenate([p[:, :h], p[:, h:]], axis=0)


def split3(x):
    a = x.astype(BF16).astype(F32)
    y = x - a
    b = y.astype(BF16).astype(F32)
    return a, b, (y - b).astype(BF16).astype(F32)


def features(xyz):
    x, y, z = xyz[0:1], xyz[1:2], xyz[2:3]
    norm = C2 * (x * x + y * y + z * z)
    n = split3(norm)
    m = [split3(-2.0 * C2 * v) for v in (x, y, z)]
    one = jnp.ones_like(x)
    zero = jnp.zeros_like(x)
    tgt = [x, y, z] * 3 + list(n) + [one] * 3 + [zero]
    src = [m[c][part] for part in range(3) for c in range(3)] + [one] * 3 + list(n) + [zero]
    row = lax.broadcasted_iota(jnp.int32, (16, xyz.shape[1]), 0)

    def build(rows):
        out = jnp.zeros((16, xyz.shape[1]), F32)
        for i, v in enumerate(rows[:15]):
            out = jnp.where(row == i, v, out)
        return out.astype(BF16)

    return build(tgt), build(src)


def up_levels(leaves, values, weights):
    out = list(values)
    start, breadth = 0, leaves
    while breadth > 1:
        for i in range(breadth // 2):
            left, right = start + 2 * i, start + 2 * i + 1
            out.append(dot2(out[left], weights(left)) + dot2(out[right], weights(right)))
        start += breadth
        breadth //= 2
    return out


def kernel(
    groups,
    coords_hbm,
    rhs_hbm,
    basis_hbm,
    lt_hbm,
    up_hbm,
    np_hbm,
    lp_hbm,
    nc_hbm,
    ut_hbm,
    ub_hbm,
    lb_hbm,
    out_ref,
    rhs_ref,
    basis_ref,
    lt_ref,
    coords_ref,
    up_ref,
    npv_ref,
    lpv_ref,
    nc_ref,
    np_ref,
    lp_ref,
    utv_ref,
    ub_ref,
    lb_ref,
    ege_ref,
    eg_ref,
    meta_ref,
    smeta_ref,
    lowwin_ref,
    fswin_ref,
    rhswin_ref,
    ftl_ref,
    fst_ref,
    rw_ref,
    inc_ref,
    lowbuf_ref,
    req_ref,
    root_ref,
    tab_ref,
    send2_ref,
    recv2_ref,
    s_ref,
    pr_ref,
    send3_ref,
    recv3_ref,
    tabd_ref,
    send4_ref,
    recv4_ref,
    oh3_ref,
    loc_sem,
    halo_s,
    halo_r,
    req_s,
    req_r,
    p1_s,
    p1_r,
    p2_s,
    p2_r,
    p3_s,
    p3_r,
    p4_s,
    p4_r,
):
    ndev = groups * MEMB
    depth = ndev.bit_length() - 1
    subs = lax.axis_size("sub")
    dev = lax.axis_index("grp") * subs + lax.axis_index("sub")
    g = dev // MEMB
    m = dev % MEMB
    leaves = rhs_hbm.shape[1] // LEAF
    low_count = 2 * leaves - 2
    near_cap = npv_ref.shape[1]
    low_dev = lpv_ref.shape[1]

    def at_dev(d):
        return (d // subs, d % subs)

    def other_group(i):
        return ((g + i) % groups) * MEMB + m

    def other_member(i):
        return g * MEMB + (m + i) % MEMB

    fetched = []
    for j, (src, dst) in enumerate((
        (rhs_hbm, rhs_ref),
        (basis_hbm, basis_ref),
        (lt_hbm, lt_ref),
        (up_hbm, up_ref),
        (coords_hbm, coords_ref),
        (np_hbm, npv_ref),
        (lp_hbm, lpv_ref),
        (nc_hbm, nc_ref),
        (np_hbm, np_ref),
        (lp_hbm, lp_ref),
        (ut_hbm, utv_ref),
        (ub_hbm, ub_ref),
        (lb_hbm, lb_ref),
    )):
        fetched.append(pltpu.make_async_copy(src, dst, loc_sem.at[j + 1]))
        fetched[-1].start()

    barrier = pltpu.get_barrier_semaphore()


    def greet(to):
        def body(i, c):
            pl.semaphore_signal(barrier, inc=1, device_id=at_dev(to(i)), device_id_type=MESH)
            return c

        return body

    after, before = (dev + 1) % ndev, (dev + ndev - 1) % ndev
    lax.fori_loop(1, groups, greet(other_group), 0)
    lax.fori_loop(1, MEMB, greet(other_member), 0)
    for d in (after, before):
        pl.semaphore_signal(barrier, inc=1, device_id=at_dev(d), device_id_type=MESH)

    def start(copy, count):
        def body(i, c):
            copy(i).start()
            return c

        lax.fori_loop(1, count, body, 0)

    def await_recv(copy, count):
        def body(i, c):
            copy(i).wait_recv()
            return c

        lax.fori_loop(1, count, body, 0)

    def await_send(copy, count):
        def body(i, c):
            copy(i).wait_send()
            return c

        lax.fori_loop(1, count, body, 0)

    def remote(src, dst, send, recv, to):
        return pltpu.make_async_remote_copy(src, dst, send, recv, device_id=at_dev(to), device_id_type=MESH)

    for c in fetched[:3]:
        c.wait()
    first = [
        dot(rhs_ref[:, l * LEAF : (l + 1) * LEAF], basis_ref[:, l * LEAF : (l + 1) * LEAF], nt=True)
        for l in range(leaves)
    ]
    low = up_levels(leaves, first, lambda i: lt_ref[i])
    root_ref[m] = pack(low[-1]).astype(BF16)

    def column(row):
        wide = jnp.concatenate([row, jnp.full((1, 128 - row.shape[1]), -1, jnp.int32)], axis=1)
        return wide, jnp.transpose(jnp.broadcast_to(wide, (128, 128)))

    fetched[3].wait()
    slane = lax.broadcasted_iota(jnp.int32, (8, 128), 1)
    req_ref[g] = jnp.where(slane < 64, column(up_ref[1:2, :])[1][:8], column(up_ref[0:1, :])[1][:8])

    pl.semaphore_wait(barrier, groups - 1 + MEMB - 1 + 2)

    def copy1(i):
        return remote(root_ref.at[m], root_ref.at[m], p1_s.at[i], p1_r.at[i], other_member(i))

    def copy_req(i):
        return remote(req_ref.at[g], req_ref.at[g], req_s.at[i], req_r.at[i], other_group(i))

    start(copy1, MEMB)
    start(copy_req, groups)

    tab_ref[:, MEMB * 8 :, :] = jnp.zeros((2, (ROWS - MEMB) * 8, 128), F32)
    for i in range(low_count):
        lowwin_ref[low_count + i] = pack(low[i])
    for c in fetched[4:8]:
        c.wait()
    ft, fs = features(coords_ref[...].astype(F32))
    fswin_ref[1] = fs
    for l in range(leaves):
        ftl_ref[l] = ft[:, l * LEAF : (l + 1) * LEAF]
    halo = []
    for side, to in ((0, after), (1, before)):
        for j, (src, dst) in enumerate((
            (fswin_ref.at[1], fswin_ref.at[2 * side]),
            (rhs_ref, rhswin_ref.at[2 * side]),
            (lowwin_ref.at[pl.ds(low_count, low_count)], lowwin_ref.at[pl.ds(2 * side * low_count, low_count)]),
        )):
            k = j * 2 + side
            halo.append(remote(src, dst, halo_s.at[k], halo_r.at[k], to))

    def chain(pairs, live, first_target, targets):
        t, down = column(pairs[0:1, :] - first_target)
        slot = lax.broadcasted_iota(jnp.int32, (128, 128), 0)
        lane = lax.broadcasted_iota(jnp.int32, (128, 128), 1)
        ok = slot < live
        prev = jnp.max(jnp.where(ok & (slot < lane) & (down == t), slot + 1, 0), axis=0, keepdims=True)
        last = jnp.max(jnp.where(ok & (down == lane) & (lane < targets), slot + 1, 0), axis=0, keepdims=True)
        return prev, last

    rows = chain(npv_ref[...], nc_ref[...], dev * leaves, leaves) + chain(lpv_ref[...], low_dev, dev * low_count, low_count)
    meta_ref[...] = jnp.concatenate(list(rows) + [jnp.zeros((4, 128), jnp.int32)], axis=0)
    to_scalar = pltpu.make_async_copy(meta_ref, smeta_ref, loc_sem.at[0])
    to_scalar.start()

    def row_ids(trow):
        ids = jnp.full(trow.shape, -1, jnp.int32)
        row = 0
        for level in range(depth):
            base = 2 * ndev - 2 * (ndev >> level)
            count = max(1, MEMB >> level)
            at = base + (g * count if level <= 4 else g // (1 << (level - 4)))
            ids = jnp.where((trow >= row) & (trow < row + count), at + trow - row, ids)
            row += count
        return ids

    clusters = utv_ref.shape[2]
    pick = lax.broadcasted_iota(jnp.int32, (ROWS, clusters), 1) == row_ids(
        lax.broadcasted_iota(jnp.int32, (ROWS, clusters), 0)
    )
    pick = jnp.where(pick, 1.0, 0.0).astype(BF16)
    for c in fetched[8:]:
        c.wait()
    for i in range(32):
        x = jnp.concatenate([utv_ref[i], utv_ref[i + 32]], axis=0)
        ege_ref[i * ROWS : (i + 1) * ROWS, :] = dot(pick, x, nt=True)
    used = 2 * MEMB - 1 + depth - 5
    for c in range(used):
        eg_ref[c] = unpack(ege_ref[pl.ds(c, 32, stride=ROWS), :]).astype(BF16)

    await_recv(copy_req, groups)
    lane = lax.broadcasted_iota(jnp.int32, (1, 2 * ROWS), 1)
    half = lane // ROWS
    cid = row_ids(lane % ROWS)

    def onehot(column):
        pieces = []
        for other in range(groups):
            eq = (column[other] == cid).astype(F32)
            for part in range(2):
                pieces.append(jnp.where(half == part, eq, 0.0))
        return jnp.concatenate(pieces, axis=0)

    req = req_ref[...]
    oh2 = onehot([req[o][:, 0:1] for o in range(groups)]).astype(BF16)
    oh3_ref[...] = jnp.transpose(onehot([req[o][:, 64:65] for o in range(groups)])).astype(BF16)

    def copy2(h):
        def copy(i):
            part = pl.ds(h * 64, 64)
            return remote(
                send2_ref.at[(g + i) % groups, part], recv2_ref.at[g, part], p2_s.at[h, i], p2_r.at[h, i], other_group(i)
            )

        return copy

    def climb(h):
        roots = [root_ref[i].astype(F32)[h * 8 : h * 8 + 8] for i in range(MEMB)]
        for i in range(MEMB):
            tab_ref[h, i * 8 : i * 8 + 8, :] = roots[i]
        table = up_levels(MEMB, [unpack(r) for r in roots], lambda i: eg_ref[i])
        for level in range(5, depth):
            table.append(dot2(table[-1], eg_ref[len(table) - 1]))
        for i in range(MEMB, len(table)):
            tab_ref[h, i * 8 : i * 8 + 8, :] = pack(table[i])
        for b in range(h * 4, h * 4 + 4):
            t = jnp.concatenate([tab_ref[h, pl.ds(2 * b + vs - 8 * h, ROWS, stride=8), :] for vs in range(2)], axis=0)
            out = dot(oh2, t.astype(BF16)).astype(BF16)
            send2_ref[:, b * 16 : (b + 1) * 16, :] = out.reshape(groups, 16, 128)
        part = pl.ds(h * 64, 64)
        recv2_ref[g, part] = send2_ref[g, part]
        start(copy2(h), groups)

    for c in halo:
        c.start()
    await_recv(copy1, MEMB)
    climb(0)
    climb(1)

    to_scalar.wait()
    for c in halo:
        c.wait_recv()
    inc_ref[0] = jnp.zeros(inc_ref.shape[1:], F32)
    for w in range(3):
        for l in range(leaves):
            cols = slice(l * LEAF, (l + 1) * LEAF)
            fst_ref[w * leaves + l] = jnp.transpose(fswin_ref[w, :, cols].astype(F32)).astype(BF16)
            rw_ref[w * leaves + l] = rhs_ref[:, cols] if w == 1 else rhswin_ref[w, :, cols]

    def near(lo, hi):
        def body(b, c):
            made = []
            for u in range(UNROLL):
                k = b * UNROLL + u
                t = jnp.clip(np_ref[0, k] - dev * leaves, 0, leaves - 1)
                s = jnp.clip(np_ref[1, k] - (dev - 1) * leaves, 0, 3 * leaves - 1)
                sq = jnp.maximum(dot(fst_ref[s], ftl_ref[t]), 1e-30)
                p = sq * lax.rsqrt(sq)
                tile = ((AMP + (AMP * LN2) * p) * jnp.exp2(-p)).astype(BF16)
                made.append(dot(rw_ref[s], tile))
            for u in range(UNROLL):
                k = b * UNROLL + u
                inc_ref[k + 1] = made[u] + inc_ref[smeta_ref[0, k]]
            return c

        lax.fori_loop(lo // UNROLL, hi // UNROLL, body, 0)

    def copy3(h):
        def copy(i):
            part = pl.ds(h * 64, 64)
            return remote(send3_ref.at[part], recv3_ref.at[g, part], p3_s.at[h, i], p3_r.at[h, i], other_group(i))

        return copy

    def couple(h):
        part = pl.ds(h * 64, 64)
        total = recv2_ref[0, part].astype(F32)
        for o in range(1, groups):
            total = total + recv2_ref[o, part].astype(F32)
        s_ref[part, :] = total
        for i in range(8):
            x = s_ref[pl.ds(h * 64 + i, 8, stride=8), :]
            pr_ref[h * 64 + i * 8 : h * 64 + i * 8 + 8, :] = pack(dot2(unpack(x), ub_ref[i], nt=True))
        made = jnp.concatenate([pr_ref[pl.ds(h * 64 + v, 8, stride=8), :] for v in range(8)], axis=0).astype(BF16)
        send3_ref[part, :] = made
        recv3_ref[g, part] = made
        start(copy3(h), groups)

    def copy4(h):
        def copy(i):
            part = pl.ds(h * 8, 8)
            return remote(
                send4_ref.at[(m + i) % MEMB, part], recv4_ref.at[m, part], p4_s.at[h, i], p4_r.at[h, i], other_member(i)
            )

        return copy

    def descend(h):
        oh3 = oh3_ref[...]
        for b in range(h * 4, h * 4 + 4):
            r = recv3_ref[:, b * 16 : (b + 1) * 16, :].reshape(groups * 16, 128)
            tabd_ref[b * 2 * ROWS : (b + 1) * 2 * ROWS, :] = dot(oh3, r)

        def summed(c):
            return unpack(tabd_ref[pl.ds(h * 8 * ROWS + c, 8, stride=ROWS), :])

        at = used - 1
        down = summed(at)
        while at > 2 * MEMB - 2:
            at -= 1
            down = summed(at) + dot2(down, eg_ref[at], nt=True)
        current = [down]
        breadth = 2
        while breadth <= MEMB:
            at = 2 * MEMB - 2 * breadth
            current = [summed(at + i) + dot2(current[i // 2], eg_ref[at + i], nt=True) for i in range(breadth)]
            breadth *= 2
        for i in range(MEMB):
            send4_ref[i, h * 8 : h * 8 + 8] = pack(current[i])
        part = pl.ds(h * 8, 8)
        recv4_ref[m, part] = send4_ref[m, part]
        start(copy4(h), MEMB)

    def finish(h):
        part = pl.ds(h * 8, 8)
        total = recv4_ref[0, part]
        for i in range(1, MEMB):
            total = total + recv4_ref[i, part]
        current = [unpack(total)]
        lower, upper = slice(h * 8, h * 8 + 8), slice(16 + h * 8, 24 + h * 8)
        breadth = 2
        while breadth <= leaves:
            at = 2 * leaves - 2 * breadth
            grown = []
            for i in range(breadth):
                last = smeta_ref[3, at + i]
                own = jnp.concatenate([lowbuf_ref[last, lower], lowbuf_ref[last, upper]], axis=0)
                grown.append(own + dot2(current[i // 2], lt_ref[at + i], nt=True))
            current = grown
            breadth *= 2
        for l in range(leaves):
            cols = slice(l * LEAF, (l + 1) * LEAF)
            far = dot2(current[l], basis_ref[:, cols])
            last = smeta_ref[1, l]
            out_ref[lower, cols] = inc_ref[last, lower] + far[:8]
            out_ref[upper, cols] = inc_ref[last, upper] + far[8:]

    near(0, CUT[0])
    await_recv(copy2(0), groups)
    couple(0)
    near(CUT[0], CUT[1])
    await_recv(copy2(1), groups)
    couple(1)
    near(CUT[1], CUT[2])
    await_recv(copy3(0), groups)
    descend(0)
    near(CUT[2], CUT[3])
    await_recv(copy3(1), groups)
    descend(1)

    lowbuf_ref[0] = jnp.zeros(lowbuf_ref.shape[1:], F32)
    made = []
    for k in range(low_dev):
        s = jnp.clip(lp_ref[1, k] - (dev - 1) * low_count, 0, 3 * low_count - 1)
        made.append(dot2(unpack(lowwin_ref[s]), lb_ref[k], nt=True))
    for k in range(low_dev):
        lowbuf_ref[k + 1] = made[k] + lowbuf_ref[smeta_ref[2, k]]
    near(CUT[3], near_cap)

    for h in range(2):
        await_recv(copy4(h), MEMB)
        finish(h)
    for c in halo:
        c.wait_send()
    await_send(copy_req, groups)
    await_send(copy1, MEMB)
    for h in range(2):
        await_send(copy2(h), groups)
        await_send(copy3(h), groups)
        await_send(copy4(h), MEMB)


def on_device(coords, rhs, basis, lt, lp, lb, ut, up, ub, npairs, ncount):
    ndev = lax.axis_size(("grp", "sub"))
    groups = ndev // MEMB
    points = rhs.shape[1]
    leaves = points // LEAF
    low_count = 2 * leaves - 2
    near_cap = npairs.shape[1]
    vm = pl.BlockSpec(memory_space=pltpu.VMEM)
    anym = pl.BlockSpec(memory_space=pl.ANY)
    dma = pltpu.SemaphoreType.DMA
    ut = jnp.transpose(ut, (1, 2, 0))
    return pl.pallas_call(
        lambda *refs: kernel(groups, *refs),
        out_shape=jax.ShapeDtypeStruct((32, points), F32),
        in_specs=[anym] * 11,
        out_specs=vm,
        scratch_shapes=[
            pltpu.VMEM(rhs.shape, BF16),
            pltpu.VMEM(basis.shape, BF16),
            pltpu.VMEM(lt.shape, BF16),
            pltpu.VMEM(coords.shape, BF16),
            pltpu.VMEM(up.shape, jnp.int32),
            pltpu.VMEM(npairs.shape, jnp.int32),
            pltpu.VMEM(lp.shape, jnp.int32),
            pltpu.VMEM((1, 1), jnp.int32),
            pltpu.SMEM(npairs.shape, jnp.int32),
            pltpu.SMEM(lp.shape, jnp.int32),
            pltpu.VMEM(ut.shape, BF16),
            pltpu.VMEM(ub.shape, BF16),
            pltpu.VMEM(lb.shape, BF16),
            pltpu.VMEM((32 * ROWS, 128), F32),
            pltpu.VMEM((ROWS, 64, 64), BF16),
            pltpu.VMEM((8, 128), jnp.int32),
            pltpu.SMEM((8, 128), jnp.int32),
            pltpu.VMEM((3 * low_count, 16, 128), F32),
            pltpu.VMEM((3, 16, points), BF16),
            pltpu.VMEM((3, 32, points), BF16),
            pltpu.VMEM((leaves, 16, LEAF), BF16),
            pltpu.VMEM((3 * leaves, LEAF, 16), BF16),
            pltpu.VMEM((3 * leaves, 32, LEAF), BF16),
            pltpu.VMEM((near_cap + 1, 32, LEAF), F32),
            pltpu.VMEM((lp.shape[1] + 1, 32, 64), F32),
            pltpu.VMEM((groups, 8, 128), jnp.int32),
            pltpu.VMEM((MEMB, 16, 128), BF16),
            pltpu.VMEM((2, ROWS * 8, 128), F32),
            pltpu.VMEM((groups, 128, 128), BF16),
            pltpu.VMEM((groups, 128, 128), BF16),
            pltpu.VMEM((128, 128), F32),
            pltpu.VMEM((128, 128), F32),
            pltpu.VMEM((128, 128), BF16),
            pltpu.VMEM((groups, 128, 128), BF16),
            pltpu.VMEM((8 * 2 * ROWS, 128), F32),
            pltpu.VMEM((MEMB, 16, 128), F32),
            pltpu.VMEM((MEMB, 16, 128), F32),
            pltpu.VMEM((2 * ROWS, groups * 16), BF16),
            dma((14,)),
            dma((6,)),
            dma((6,)),
            dma((groups,)),
            dma((groups,)),
            dma((MEMB,)),
            dma((MEMB,)),
            dma((2, groups)),
            dma((2, groups)),
            dma((2, groups)),
            dma((2, groups)),
            dma((2, MEMB)),
            dma((2, MEMB)),
        ],
        compiler_params=pltpu.CompilerParams(
            collective_id=0, has_side_effects=True, vmem_limit_bytes=56 * 2**20
        ),
        name="tree_product",
    )(coords, rhs, basis, lt, up, npairs, lp, ncount.reshape(1, 1), ut, ub, lb)


def solution(mesh):
    both = ("grp", "sub")
    in_specs = (
        P(None, both), P(None, both), P(None, both), P(both), P(None, both), P(both),
        P(), P(None, both), P(both), P(None, both), P(both),
    )
    return jax.shard_map(on_device, mesh=mesh, in_specs=in_specs, out_specs=P(None, both), check_vma=False)
```

```python
import jax
import jax.numpy as jnp
from jax import lax
from jax.experimental import pallas as pl
from jax.experimental.pallas import tpu as pltpu
from jax.sharding import PartitionSpec as P

LEAF = 256
MEMB = 16
ROWS = 40
C2 = 6.244106943016823
AMP = 0.0625
LN2 = 0.6931471805599453
UNROLL = 8
CUT = (24, 24, 56, 56)
MESH = pl.DeviceIdType.MESH
F32 = jnp.float32
BF16 = jnp.bfloat16


def dot(a, b, nt=False):
    dims = (((1,), (1,)), ((), ())) if nt else (((1,), (0,)), ((), ()))
    return lax.dot_general(a, b, dims, preferred_element_type=F32)


def split2(c):
    hi = c.astype(BF16)
    lo = (c - hi.astype(F32)).astype(BF16)
    return jnp.concatenate([hi, lo], axis=0)


def dot2(c, w, nt=False):
    n = c.shape[0]
    r = dot(split2(c), w, nt)
    return r[:n] + r[n:]


def pack(c):
    h = c.shape[0] // 2
    return jnp.concatenate([c[:h], c[h:]], axis=1)


def unpack(p):
    h = p.shape[1] // 2
    return jnp.concatenate([p[:, :h], p[:, h:]], axis=0)


def split3(x):
    a = x.astype(BF16).astype(F32)
    y = x - a
    b = y.astype(BF16).astype(F32)
    return a, b, (y - b).astype(BF16).astype(F32)


def features(xyz):
    x, y, z = xyz[0:1], xyz[1:2], xyz[2:3]
    norm = C2 * (x * x + y * y + z * z)
    n = split3(norm)
    m = [split3(-2.0 * C2 * v) for v in (x, y, z)]
    one = jnp.ones_like(x)
    zero = jnp.zeros_like(x)
    tgt = [x, y, z] * 3 + list(n) + [one] * 3 + [zero]
    src = [m[c][part] for part in range(3) for c in range(3)] + [one] * 3 + list(n) + [zero]
    row = lax.broadcasted_iota(jnp.int32, (16, xyz.shape[1]), 0)

    def build(rows):
        out = jnp.zeros((16, xyz.shape[1]), F32)
        for i, v in enumerate(rows[:15]):
            out = jnp.where(row == i, v, out)
        return out.astype(BF16)

    return build(tgt), build(src)


def up_levels(leaves, values, weights):
    out = list(values)
    start, breadth = 0, leaves
    while breadth > 1:
        for i in range(breadth // 2):
            left, right = start + 2 * i, start + 2 * i + 1
            out.append(dot2(out[left], weights(left)) + dot2(out[right], weights(right)))
        start += breadth
        breadth //= 2
    return out


def kernel(
    groups,
    coords_hbm,
    rhs_hbm,
    basis_hbm,
    lt_hbm,
    up_hbm,
    np_hbm,
    lp_hbm,
    nc_hbm,
    ut_hbm,
    ub_hbm,
    lb_hbm,
    out_ref,
    rhs_ref,
    basis_ref,
    lt_ref,
    coords_ref,
    up_ref,
    npv_ref,
    lpv_ref,
    nc_ref,
    np_ref,
    lp_ref,
    utv_ref,
    ub_ref,
    lb_ref,
    ege_ref,
    eg_ref,
    meta_ref,
    smeta_ref,
    lowwin_ref,
    fswin_ref,
    rhswin_ref,
    ftl_ref,
    fst_ref,
    rw_ref,
    inc_ref,
    lowbuf_ref,
    req_ref,
    root_ref,
    tab_ref,
    send2_ref,
    recv2_ref,
    s_ref,
    pr_ref,
    send3_ref,
    recv3_ref,
    tabd_ref,
    send4_ref,
    recv4_ref,
    oh3_ref,
    loc_sem,
    halo_s,
    halo_r,
    req_s,
    req_r,
    p1_s,
    p1_r,
    p2_s,
    p2_r,
    p3_s,
    p3_r,
    p4_s,
    p4_r,
):
    ndev = groups * MEMB
    depth = ndev.bit_length() - 1
    subs = lax.axis_size("sub")
    dev = lax.axis_index("grp") * subs + lax.axis_index("sub")
    g = dev // MEMB
    m = dev % MEMB
    leaves = rhs_hbm.shape[1] // LEAF
    low_count = 2 * leaves - 2
    near_cap = npv_ref.shape[1]
    low_dev = lpv_ref.shape[1]

    def at_dev(d):
        return (d // subs, d % subs)

    def other_group(i):
        return ((g + i) % groups) * MEMB + m

    def other_member(i):
        return g * MEMB + (m + i) % MEMB

    fetched = []
    for j, (src, dst) in enumerate((
        (rhs_hbm, rhs_ref),
        (basis_hbm, basis_ref),
        (lt_hbm, lt_ref),
        (up_hbm, up_ref),
        (coords_hbm, coords_ref),
        (np_hbm, npv_ref),
        (lp_hbm, lpv_ref),
        (nc_hbm, nc_ref),
        (np_hbm, np_ref),
        (lp_hbm, lp_ref),
        (ut_hbm, utv_ref),
        (ub_hbm, ub_ref),
        (lb_hbm, lb_ref),
    )):
        fetched.append(pltpu.make_async_copy(src, dst, loc_sem.at[j + 1]))
        fetched[-1].start()

    barrier = pltpu.get_barrier_semaphore()


    def greet(to):
        def body(i, c):
            pl.semaphore_signal(barrier, inc=1, device_id=at_dev(to(i)), device_id_type=MESH)
            return c

        return body

    after, before = (dev + 1) % ndev, (dev + ndev - 1) % ndev
    lax.fori_loop(1, groups, greet(other_group), 0)
    lax.fori_loop(1, MEMB, greet(other_member), 0)
    for d in (after, before):
        pl.semaphore_signal(barrier, inc=1, device_id=at_dev(d), device_id_type=MESH)

    def start(copy, count):
        def body(i, c):
            copy(i).start()
            return c

        lax.fori_loop(1, count, body, 0)

    def await_recv(copy, count):
        def body(i, c):
            copy(i).wait_recv()
            return c

        lax.fori_loop(1, count, body, 0)

    def await_send(copy, count):
        def body(i, c):
            copy(i).wait_send()
            return c

        lax.fori_loop(1, count, body, 0)

    def remote(src, dst, send, recv, to):
        return pltpu.make_async_remote_copy(src, dst, send, recv, device_id=at_dev(to), device_id_type=MESH)

    for c in fetched[:3]:
        c.wait()
    first = [
        dot(rhs_ref[:, l * LEAF : (l + 1) * LEAF], basis_ref[:, l * LEAF : (l + 1) * LEAF], nt=True)
        for l in range(leaves)
    ]
    low = up_levels(leaves, first, lambda i: lt_ref[i])
    root_ref[m] = pack(low[-1]).astype(BF16)

    def column(row):
        wide = jnp.concatenate([row, jnp.full((1, 128 - row.shape[1]), -1, jnp.int32)], axis=1)
        return wide, jnp.transpose(jnp.broadcast_to(wide, (128, 128)))

    fetched[3].wait()
    slane = lax.broadcasted_iota(jnp.int32, (8, 128), 1)
    req_ref[g] = jnp.where(slane < 64, column(up_ref[1:2, :])[1][:8], column(up_ref[0:1, :])[1][:8])

    pl.semaphore_wait(barrier, groups - 1 + MEMB - 1 + 2)

    def copy1(i):
        return remote(root_ref.at[m], root_ref.at[m], p1_s.at[i], p1_r.at[i], other_member(i))

    def copy_req(i):
        return remote(req_ref.at[g], req_ref.at[g], req_s.at[i], req_r.at[i], other_group(i))

    start(copy1, MEMB)
    start(copy_req, groups)

    tab_ref[:, MEMB * 8 :, :] = jnp.zeros((2, (ROWS - MEMB) * 8, 128), F32)
    for i in range(low_count):
        lowwin_ref[low_count + i] = pack(low[i])
    for c in fetched[4:8]:
        c.wait()
    ft, fs = features(coords_ref[...].astype(F32))
    fswin_ref[1] = fs
    for l in range(leaves):
        ftl_ref[l] = ft[:, l * LEAF : (l + 1) * LEAF]
    halo = []
    for side, to in ((0, after), (1, before)):
        for j, (src, dst) in enumerate((
            (fswin_ref.at[1], fswin_ref.at[2 * side]),
            (rhs_ref, rhswin_ref.at[2 * side]),
            (lowwin_ref.at[pl.ds(low_count, low_count)], lowwin_ref.at[pl.ds(2 * side * low_count, low_count)]),
        )):
            k = j * 2 + side
            halo.append(remote(src, dst, halo_s.at[k], halo_r.at[k], to))

    for c in halo:
        c.start()

    def chain(pairs, live, first_target, targets):
        t, down = column(pairs[0:1, :] - first_target)
        slot = lax.broadcasted_iota(jnp.int32, (128, 128), 0)
        lane = lax.broadcasted_iota(jnp.int32, (128, 128), 1)
        ok = slot < live
        prev = jnp.max(jnp.where(ok & (slot < lane) & (down == t), slot + 1, 0), axis=0, keepdims=True)
        last = jnp.max(jnp.where(ok & (down == lane) & (lane < targets), slot + 1, 0), axis=0, keepdims=True)
        return prev, last

    rows = chain(npv_ref[...], nc_ref[...], dev * leaves, leaves) + chain(lpv_ref[...], low_dev, dev * low_count, low_count)
    meta_ref[...] = jnp.concatenate(list(rows) + [jnp.zeros((4, 128), jnp.int32)], axis=0)
    to_scalar = pltpu.make_async_copy(meta_ref, smeta_ref, loc_sem.at[0])
    to_scalar.start()

    def row_ids(trow):
        ids = jnp.full(trow.shape, -1, jnp.int32)
        row = 0
        for level in range(depth):
            base = 2 * ndev - 2 * (ndev >> level)
            count = max(1, MEMB >> level)
            at = base + (g * count if level <= 4 else g // (1 << (level - 4)))
            ids = jnp.where((trow >= row) & (trow < row + count), at + trow - row, ids)
            row += count
        return ids

    clusters = utv_ref.shape[2]
    pick = lax.broadcasted_iota(jnp.int32, (ROWS, clusters), 1) == row_ids(
        lax.broadcasted_iota(jnp.int32, (ROWS, clusters), 0)
    )
    pick = jnp.where(pick, 1.0, 0.0).astype(BF16)
    for c in fetched[8:]:
        c.wait()
    for i in range(32):
        x = jnp.concatenate([utv_ref[i], utv_ref[i + 32]], axis=0)
        ege_ref[i * ROWS : (i + 1) * ROWS, :] = dot(pick, x, nt=True)
    used = 2 * MEMB - 1 + depth - 5
    for c in range(used):
        eg_ref[c] = unpack(ege_ref[pl.ds(c, 32, stride=ROWS), :]).astype(BF16)

    await_recv(copy_req, groups)
    lane = lax.broadcasted_iota(jnp.int32, (1, 2 * ROWS), 1)
    half = lane // ROWS
    cid = row_ids(lane % ROWS)

    def onehot(column):
        pieces = []
        for other in range(groups):
            eq = (column[other] == cid).astype(F32)
            for part in range(2):
                pieces.append(jnp.where(half == part, eq, 0.0))
        return jnp.concatenate(pieces, axis=0)

    req = req_ref[...]
    oh2 = onehot([req[o][:, 0:1] for o in range(groups)]).astype(BF16)
    oh3_ref[...] = jnp.transpose(onehot([req[o][:, 64:65] for o in range(groups)])).astype(BF16)

    def copy2(h):
        def copy(i):
            part = pl.ds(h * 64, 64)
            return remote(
                send2_ref.at[(g + i) % groups, part], recv2_ref.at[g, part], p2_s.at[h, i], p2_r.at[h, i], other_group(i)
            )

        return copy

    def climb(h):
        roots = [root_ref[i].astype(F32)[h * 8 : h * 8 + 8] for i in range(MEMB)]
        for i in range(MEMB):
            tab_ref[h, i * 8 : i * 8 + 8, :] = roots[i]
        table = up_levels(MEMB, [unpack(r) for r in roots], lambda i: eg_ref[i])
        for level in range(5, depth):
            table.append(dot2(table[-1], eg_ref[len(table) - 1]))
        for i in range(MEMB, len(table)):
            tab_ref[h, i * 8 : i * 8 + 8, :] = pack(table[i])
        for b in range(h * 4, h * 4 + 4):
            t = jnp.concatenate([tab_ref[h, pl.ds(2 * b + vs - 8 * h, ROWS, stride=8), :] for vs in range(2)], axis=0)
            out = dot(oh2, t.astype(BF16)).astype(BF16)
            send2_ref[:, b * 16 : (b + 1) * 16, :] = out.reshape(groups, 16, 128)
        part = pl.ds(h * 64, 64)
        recv2_ref[g, part] = send2_ref[g, part]
        start(copy2(h), groups)

    await_recv(copy1, MEMB)
    climb(0)
    climb(1)

    to_scalar.wait()
    for c in halo:
        c.wait_recv()
    inc_ref[0] = jnp.zeros(inc_ref.shape[1:], F32)
    for w in range(3):
        for l in range(leaves):
            cols = slice(l * LEAF, (l + 1) * LEAF)
            fst_ref[w * leaves + l] = jnp.transpose(fswin_ref[w, :, cols].astype(F32)).astype(BF16)
            rw_ref[w * leaves + l] = rhs_ref[:, cols] if w == 1 else rhswin_ref[w, :, cols]

    def near(lo, hi):
        def body(b, c):
            made = []
            for u in range(UNROLL):
                k = b * UNROLL + u
                t = jnp.clip(np_ref[0, k] - dev * leaves, 0, leaves - 1)
                s = jnp.clip(np_ref[1, k] - (dev - 1) * leaves, 0, 3 * leaves - 1)
                sq = jnp.maximum(dot(fst_ref[s], ftl_ref[t]), 1e-30)
                p = sq * lax.rsqrt(sq)
                tile = ((AMP + (AMP * LN2) * p) * jnp.exp2(-p)).astype(BF16)
                made.append(dot(rw_ref[s], tile))
            for u in range(UNROLL):
                k = b * UNROLL + u
                inc_ref[k + 1] = made[u] + inc_ref[smeta_ref[0, k]]
            return c

        lax.fori_loop(lo // UNROLL, hi // UNROLL, body, 0)

    def copy3(h):
        def copy(i):
            part = pl.ds(h * 64, 64)
            return remote(send3_ref.at[part], recv3_ref.at[g, part], p3_s.at[h, i], p3_r.at[h, i], other_group(i))

        return copy

    def couple(h):
        part = pl.ds(h * 64, 64)
        total = recv2_ref[0, part].astype(F32)
        for o in range(1, groups):
            total = total + recv2_ref[o, part].astype(F32)
        s_ref[part, :] = total
        for i in range(8):
            x = s_ref[pl.ds(h * 64 + i, 8, stride=8), :]
            pr_ref[h * 64 + i * 8 : h * 64 + i * 8 + 8, :] = pack(dot2(unpack(x), ub_ref[i], nt=True))
        made = jnp.concatenate([pr_ref[pl.ds(h * 64 + v, 8, stride=8), :] for v in range(8)], axis=0).astype(BF16)
        send3_ref[part, :] = made
        recv3_ref[g, part] = made
        start(copy3(h), groups)

    def copy4(h):
        def copy(i):
            part = pl.ds(h * 8, 8)
            return remote(
                send4_ref.at[(m + i) % MEMB, part], recv4_ref.at[m, part], p4_s.at[h, i], p4_r.at[h, i], other_member(i)
            )

        return copy

    def descend(h):
        oh3 = oh3_ref[...]
        for b in range(h * 4, h * 4 + 4):
            r = recv3_ref[:, b * 16 : (b + 1) * 16, :].reshape(groups * 16, 128)
            tabd_ref[b * 2 * ROWS : (b + 1) * 2 * ROWS, :] = dot(oh3, r)

        def summed(c):
            return unpack(tabd_ref[pl.ds(h * 8 * ROWS + c, 8, stride=ROWS), :])

        at = used - 1
        down = summed(at)
        while at > 2 * MEMB - 2:
            at -= 1
            down = summed(at) + dot2(down, eg_ref[at], nt=True)
        current = [down]
        breadth = 2
        while breadth <= MEMB:
            at = 2 * MEMB - 2 * breadth
            current = [summed(at + i) + dot2(current[i // 2], eg_ref[at + i], nt=True) for i in range(breadth)]
            breadth *= 2
        for i in range(MEMB):
            send4_ref[i, h * 8 : h * 8 + 8] = pack(current[i])
        part = pl.ds(h * 8, 8)
        recv4_ref[m, part] = send4_ref[m, part]
        start(copy4(h), MEMB)

    def finish(h):
        part = pl.ds(h * 8, 8)
        total = recv4_ref[0, part]
        for i in range(1, MEMB):
            total = total + recv4_ref[i, part]
        current = [unpack(total)]
        lower, upper = slice(h * 8, h * 8 + 8), slice(16 + h * 8, 24 + h * 8)
        breadth = 2
        while breadth <= leaves:
            at = 2 * leaves - 2 * breadth
            grown = []
            for i in range(breadth):
                last = smeta_ref[3, at + i]
                own = jnp.concatenate([lowbuf_ref[last, lower], lowbuf_ref[last, upper]], axis=0)
                grown.append(own + dot2(current[i // 2], lt_ref[at + i], nt=True))
            current = grown
            breadth *= 2
        for l in range(leaves):
            cols = slice(l * LEAF, (l + 1) * LEAF)
            far = dot2(current[l], basis_ref[:, cols])
            last = smeta_ref[1, l]
            out_ref[lower, cols] = inc_ref[last, lower] + far[:8]
            out_ref[upper, cols] = inc_ref[last, upper] + far[8:]

    near(0, CUT[0])
    await_recv(copy2(0), groups)
    couple(0)
    near(CUT[0], CUT[1])
    await_recv(copy2(1), groups)
    couple(1)
    near(CUT[1], CUT[2])
    await_recv(copy3(0), groups)
    descend(0)
    near(CUT[2], CUT[3])
    await_recv(copy3(1), groups)
    descend(1)

    lowbuf_ref[0] = jnp.zeros(lowbuf_ref.shape[1:], F32)
    made = []
    for k in range(low_dev):
        s = jnp.clip(lp_ref[1, k] - (dev - 1) * low_count, 0, 3 * low_count - 1)
        made.append(dot2(unpack(lowwin_ref[s]), lb_ref[k], nt=True))
    for k in range(low_dev):
        lowbuf_ref[k + 1] = made[k] + lowbuf_ref[smeta_ref[2, k]]
    near(CUT[3], near_cap)

    for h in range(2):
        await_recv(copy4(h), MEMB)
        finish(h)
    for c in halo:
        c.wait_send()
    await_send(copy_req, groups)
    await_send(copy1, MEMB)
    for h in range(2):
        await_send(copy2(h), groups)
        await_send(copy3(h), groups)
        await_send(copy4(h), MEMB)


def on_device(coords, rhs, basis, lt, lp, lb, ut, up, ub, npairs, ncount):
    ndev = lax.axis_size(("grp", "sub"))
    groups = ndev // MEMB
    points = rhs.shape[1]
    leaves = points // LEAF
    low_count = 2 * leaves - 2
    near_cap = npairs.shape[1]
    vm = pl.BlockSpec(memory_space=pltpu.VMEM)
    anym = pl.BlockSpec(memory_space=pl.ANY)
    dma = pltpu.SemaphoreType.DMA
    ut = jnp.transpose(ut, (1, 2, 0))
    return pl.pallas_call(
        lambda *refs: kernel(groups, *refs),
        out_shape=jax.ShapeDtypeStruct((32, points), F32),
        in_specs=[anym] * 11,
        out_specs=vm,
        scratch_shapes=[
            pltpu.VMEM(rhs.shape, BF16),
            pltpu.VMEM(basis.shape, BF16),
            pltpu.VMEM(lt.shape, BF16),
            pltpu.VMEM(coords.shape, BF16),
            pltpu.VMEM(up.shape, jnp.int32),
            pltpu.VMEM(npairs.shape, jnp.int32),
            pltpu.VMEM(lp.shape, jnp.int32),
            pltpu.VMEM((1, 1), jnp.int32),
            pltpu.SMEM(npairs.shape, jnp.int32),
            pltpu.SMEM(lp.shape, jnp.int32),
            pltpu.VMEM(ut.shape, BF16),
            pltpu.VMEM(ub.shape, BF16),
            pltpu.VMEM(lb.shape, BF16),
            pltpu.VMEM((32 * ROWS, 128), F32),
            pltpu.VMEM((ROWS, 64, 64), BF16),
            pltpu.VMEM((8, 128), jnp.int32),
            pltpu.SMEM((8, 128), jnp.int32),
            pltpu.VMEM((3 * low_count, 16, 128), F32),
            pltpu.VMEM((3, 16, points), BF16),
            pltpu.VMEM((3, 32, points), BF16),
            pltpu.VMEM((leaves, 16, LEAF), BF16),
            pltpu.VMEM((3 * leaves, LEAF, 16), BF16),
            pltpu.VMEM((3 * leaves, 32, LEAF), BF16),
            pltpu.VMEM((near_cap + 1, 32, LEAF), F32),
            pltpu.VMEM((lp.shape[1] + 1, 32, 64), F32),
            pltpu.VMEM((groups, 8, 128), jnp.int32),
            pltpu.VMEM((MEMB, 16, 128), BF16),
            pltpu.VMEM((2, ROWS * 8, 128), F32),
            pltpu.VMEM((groups, 128, 128), BF16),
            pltpu.VMEM((groups, 128, 128), BF16),
            pltpu.VMEM((128, 128), F32),
            pltpu.VMEM((128, 128), F32),
            pltpu.VMEM((128, 128), BF16),
            pltpu.VMEM((groups, 128, 128), BF16),
            pltpu.VMEM((8 * 2 * ROWS, 128), F32),
            pltpu.VMEM((MEMB, 16, 128), F32),
            pltpu.VMEM((MEMB, 16, 128), F32),
            pltpu.VMEM((2 * ROWS, groups * 16), BF16),
            dma((14,)),
            dma((6,)),
            dma((6,)),
            dma((groups,)),
            dma((groups,)),
            dma((MEMB,)),
            dma((MEMB,)),
            dma((2, groups)),
            dma((2, groups)),
            dma((2, groups)),
            dma((2, groups)),
            dma((2, MEMB)),
            dma((2, MEMB)),
        ],
        compiler_params=pltpu.CompilerParams(
            collective_id=0, has_side_effects=True, vmem_limit_bytes=56 * 2**20
        ),
        name="tree_product",
    )(coords, rhs, basis, lt, up, npairs, lp, ncount.reshape(1, 1), ut, ub, lb)


def solution(mesh):
    both = ("grp", "sub")
    in_specs = (
        P(None, both), P(None, both), P(None, both), P(both), P(None, both), P(both),
        P(), P(None, both), P(both), P(None, both), P(both),
    )
    return jax.shard_map(on_device, mesh=mesh, in_specs=in_specs, out_specs=P(None, both), check_vma=False)
```

```python
import jax
import jax.numpy as jnp
from jax import lax
from jax.experimental import pallas as pl
from jax.experimental.pallas import tpu as pltpu
from jax.sharding import PartitionSpec as P

LEAF = 256
MEMB = 16
ROWS = 40
C2 = 6.244106943016823
AMP = 0.0625
LN2 = 0.6931471805599453
UNROLL = 16
CUT = (32, 32, 64, 64)
MESH = pl.DeviceIdType.MESH
F32 = jnp.float32
BF16 = jnp.bfloat16


def dot(a, b, nt=False):
    dims = (((1,), (1,)), ((), ())) if nt else (((1,), (0,)), ((), ()))
    return lax.dot_general(a, b, dims, preferred_element_type=F32)


def split2(c):
    hi = c.astype(BF16)
    lo = (c - hi.astype(F32)).astype(BF16)
    return jnp.concatenate([hi, lo], axis=0)


def dot2(c, w, nt=False):
    n = c.shape[0]
    r = dot(split2(c), w, nt)
    return r[:n] + r[n:]


def pack(c):
    h = c.shape[0] // 2
    return jnp.concatenate([c[:h], c[h:]], axis=1)


def unpack(p):
    h = p.shape[1] // 2
    return jnp.concatenate([p[:, :h], p[:, h:]], axis=0)


def split3(x):
    a = x.astype(BF16).astype(F32)
    y = x - a
    b = y.astype(BF16).astype(F32)
    return a, b, (y - b).astype(BF16).astype(F32)


def features(xyz):
    x, y, z = xyz[0:1], xyz[1:2], xyz[2:3]
    norm = C2 * (x * x + y * y + z * z)
    n = split3(norm)
    m = [split3(-2.0 * C2 * v) for v in (x, y, z)]
    one = jnp.ones_like(x)
    zero = jnp.zeros_like(x)
    tgt = [x, y, z] * 3 + list(n) + [one] * 3 + [zero]
    src = [m[c][part] for part in range(3) for c in range(3)] + [one] * 3 + list(n) + [zero]
    row = lax.broadcasted_iota(jnp.int32, (16, xyz.shape[1]), 0)

    def build(rows):
        out = jnp.zeros((16, xyz.shape[1]), F32)
        for i, v in enumerate(rows[:15]):
            out = jnp.where(row == i, v, out)
        return out.astype(BF16)

    return build(tgt), build(src)


def up_levels(leaves, values, weights):
    out = list(values)
    start, breadth = 0, leaves
    while breadth > 1:
        for i in range(breadth // 2):
            left, right = start + 2 * i, start + 2 * i + 1
            out.append(dot2(out[left], weights(left)) + dot2(out[right], weights(right)))
        start += breadth
        breadth //= 2
    return out


def kernel(
    groups,
    coords_hbm,
    rhs_hbm,
    basis_hbm,
    lt_hbm,
    up_hbm,
    np_hbm,
    lp_hbm,
    nc_hbm,
    ut_hbm,
    ub_hbm,
    lb_hbm,
    out_ref,
    rhs_ref,
    basis_ref,
    lt_ref,
    coords_ref,
    up_ref,
    npv_ref,
    lpv_ref,
    nc_ref,
    np_ref,
    lp_ref,
    utv_ref,
    ub_ref,
    lb_ref,
    ege_ref,
    eg_ref,
    meta_ref,
    smeta_ref,
    lowwin_ref,
    fswin_ref,
    rhswin_ref,
    ftl_ref,
    fst_ref,
    rw_ref,
    inc_ref,
    lowbuf_ref,
    req_ref,
    root_ref,
    tab_ref,
    send2_ref,
    recv2_ref,
    s_ref,
    pr_ref,
    send3_ref,
    recv3_ref,
    tabd_ref,
    send4_ref,
    recv4_ref,
    oh3_ref,
    loc_sem,
    halo_s,
    halo_r,
    req_s,
    req_r,
    p1_s,
    p1_r,
    p2_s,
    p2_r,
    p3_s,
    p3_r,
    p4_s,
    p4_r,
):
    ndev = groups * MEMB
    depth = ndev.bit_length() - 1
    subs = lax.axis_size("sub")
    dev = lax.axis_index("grp") * subs + lax.axis_index("sub")
    g = dev // MEMB
    m = dev % MEMB
    leaves = rhs_hbm.shape[1] // LEAF
    low_count = 2 * leaves - 2
    near_cap = npv_ref.shape[1]
    low_dev = lpv_ref.shape[1]

    def at_dev(d):
        return (d // subs, d % subs)

    def other_group(i):
        return ((g + i) % groups) * MEMB + m

    def other_member(i):
        return g * MEMB + (m + i) % MEMB

    fetched = []
    for j, (src, dst) in enumerate((
        (rhs_hbm, rhs_ref),
        (basis_hbm, basis_ref),
        (lt_hbm, lt_ref),
        (up_hbm, up_ref),
        (coords_hbm, coords_ref),
        (np_hbm, npv_ref),
        (lp_hbm, lpv_ref),
        (nc_hbm, nc_ref),
        (np_hbm, np_ref),
        (lp_hbm, lp_ref),
        (ut_hbm, utv_ref),
        (ub_hbm, ub_ref),
        (lb_hbm, lb_ref),
    )):
        fetched.append(pltpu.make_async_copy(src, dst, loc_sem.at[j + 1]))
        fetched[-1].start()

    barrier = pltpu.get_barrier_semaphore()


    def greet(to):
        def body(i, c):
            pl.semaphore_signal(barrier, inc=1, device_id=at_dev(to(i)), device_id_type=MESH)
            return c

        return body

    after, before = (dev + 1) % ndev, (dev + ndev - 1) % ndev
    lax.fori_loop(1, groups, greet(other_group), 0)
    lax.fori_loop(1, MEMB, greet(other_member), 0)
    for d in (after, before):
        pl.semaphore_signal(barrier, inc=1, device_id=at_dev(d), device_id_type=MESH)

    def start(copy, count):
        def body(i, c):
            copy(i).start()
            return c

        lax.fori_loop(1, count, body, 0)

    def await_recv(copy, count):
        def body(i, c):
            copy(i).wait_recv()
            return c

        lax.fori_loop(1, count, body, 0)

    def await_send(copy, count):
        def body(i, c):
            copy(i).wait_send()
            return c

        lax.fori_loop(1, count, body, 0)

    def remote(src, dst, send, recv, to):
        return pltpu.make_async_remote_copy(src, dst, send, recv, device_id=at_dev(to), device_id_type=MESH)

    for c in fetched[:3]:
        c.wait()
    first = [
        dot(rhs_ref[:, l * LEAF : (l + 1) * LEAF], basis_ref[:, l * LEAF : (l + 1) * LEAF], nt=True)
        for l in range(leaves)
    ]
    low = up_levels(leaves, first, lambda i: lt_ref[i])
    root_ref[m] = pack(low[-1]).astype(BF16)

    def column(row):
        wide = jnp.concatenate([row, jnp.full((1, 128 - row.shape[1]), -1, jnp.int32)], axis=1)
        return wide, jnp.transpose(jnp.broadcast_to(wide, (128, 128)))

    fetched[3].wait()
    slane = lax.broadcasted_iota(jnp.int32, (8, 128), 1)
    req_ref[g] = jnp.where(slane < 64, column(up_ref[1:2, :])[1][:8], column(up_ref[0:1, :])[1][:8])

    pl.semaphore_wait(barrier, groups - 1 + MEMB - 1 + 2)

    def copy1(i):
        return remote(root_ref.at[m], root_ref.at[m], p1_s.at[i], p1_r.at[i], other_member(i))

    def copy_req(i):
        return remote(req_ref.at[g], req_ref.at[g], req_s.at[i], req_r.at[i], other_group(i))

    start(copy1, MEMB)
    start(copy_req, groups)

    tab_ref[:, MEMB * 8 :, :] = jnp.zeros((2, (ROWS - MEMB) * 8, 128), F32)
    for i in range(low_count):
        lowwin_ref[low_count + i] = pack(low[i])
    for c in fetched[4:8]:
        c.wait()
    ft, fs = features(coords_ref[...].astype(F32))
    fswin_ref[1] = fs
    for l in range(leaves):
        ftl_ref[l] = ft[:, l * LEAF : (l + 1) * LEAF]
    halo = []
    for side, to in ((0, after), (1, before)):
        for j, (src, dst) in enumerate((
            (fswin_ref.at[1], fswin_ref.at[2 * side]),
            (rhs_ref, rhswin_ref.at[2 * side]),
            (lowwin_ref.at[pl.ds(low_count, low_count)], lowwin_ref.at[pl.ds(2 * side * low_count, low_count)]),
        )):
            k = j * 2 + side
            halo.append(remote(src, dst, halo_s.at[k], halo_r.at[k], to))

    for c in halo:
        c.start()

    def chain(pairs, live, first_target, targets):
        t, down = column(pairs[0:1, :] - first_target)
        slot = lax.broadcasted_iota(jnp.int32, (128, 128), 0)
        lane = lax.broadcasted_iota(jnp.int32, (128, 128), 1)
        ok = slot < live
        prev = jnp.max(jnp.where(ok & (slot < lane) & (down == t), slot + 1, 0), axis=0, keepdims=True)
        last = jnp.max(jnp.where(ok & (down == lane) & (lane < targets), slot + 1, 0), axis=0, keepdims=True)
        return prev, last

    rows = chain(npv_ref[...], nc_ref[...], dev * leaves, leaves) + chain(lpv_ref[...], low_dev, dev * low_count, low_count)
    meta_ref[...] = jnp.concatenate(list(rows) + [jnp.zeros((4, 128), jnp.int32)], axis=0)
    to_scalar = pltpu.make_async_copy(meta_ref, smeta_ref, loc_sem.at[0])
    to_scalar.start()

    def row_ids(trow):
        ids = jnp.full(trow.shape, -1, jnp.int32)
        row = 0
        for level in range(depth):
            base = 2 * ndev - 2 * (ndev >> level)
            count = max(1, MEMB >> level)
            at = base + (g * count if level <= 4 else g // (1 << (level - 4)))
            ids = jnp.where((trow >= row) & (trow < row + count), at + trow - row, ids)
            row += count
        return ids

    clusters = utv_ref.shape[2]
    pick = lax.broadcasted_iota(jnp.int32, (ROWS, clusters), 1) == row_ids(
        lax.broadcasted_iota(jnp.int32, (ROWS, clusters), 0)
    )
    pick = jnp.where(pick, 1.0, 0.0).astype(BF16)
    for c in fetched[8:]:
        c.wait()
    for i in range(32):
        x = jnp.concatenate([utv_ref[i], utv_ref[i + 32]], axis=0)
        ege_ref[i * ROWS : (i + 1) * ROWS, :] = dot(pick, x, nt=True)
    used = 2 * MEMB - 1 + depth - 5
    for c in range(used):
        eg_ref[c] = unpack(ege_ref[pl.ds(c, 32, stride=ROWS), :]).astype(BF16)

    await_recv(copy_req, groups)
    lane = lax.broadcasted_iota(jnp.int32, (1, 2 * ROWS), 1)
    half = lane // ROWS
    cid = row_ids(lane % ROWS)

    def onehot(column):
        pieces = []
        for other in range(groups):
            eq = (column[other] == cid).astype(F32)
            for part in range(2):
                pieces.append(jnp.where(half == part, eq, 0.0))
        return jnp.concatenate(pieces, axis=0)

    req = req_ref[...]
    oh2 = onehot([req[o][:, 0:1] for o in range(groups)]).astype(BF16)
    oh3_ref[...] = jnp.transpose(onehot([req[o][:, 64:65] for o in range(groups)])).astype(BF16)

    def copy2(h):
        def copy(i):
            part = pl.ds(h * 64, 64)
            return remote(
                send2_ref.at[(g + i) % groups, part], recv2_ref.at[g, part], p2_s.at[h, i], p2_r.at[h, i], other_group(i)
            )

        return copy

    def climb(h):
        roots = [root_ref[i].astype(F32)[h * 8 : h * 8 + 8] for i in range(MEMB)]
        for i in range(MEMB):
            tab_ref[h, i * 8 : i * 8 + 8, :] = roots[i]
        table = up_levels(MEMB, [unpack(r) for r in roots], lambda i: eg_ref[i])
        for level in range(5, depth):
            table.append(dot2(table[-1], eg_ref[len(table) - 1]))
        for i in range(MEMB, len(table)):
            tab_ref[h, i * 8 : i * 8 + 8, :] = pack(table[i])
        for b in range(h * 4, h * 4 + 4):
            t = jnp.concatenate([tab_ref[h, pl.ds(2 * b + vs - 8 * h, ROWS, stride=8), :] for vs in range(2)], axis=0)
            out = dot(oh2, t.astype(BF16)).astype(BF16)
            send2_ref[:, b * 16 : (b + 1) * 16, :] = out.reshape(groups, 16, 128)
        part = pl.ds(h * 64, 64)
        recv2_ref[g, part] = send2_ref[g, part]
        start(copy2(h), groups)

    await_recv(copy1, MEMB)
    climb(0)
    climb(1)

    to_scalar.wait()
    for c in halo:
        c.wait_recv()
    inc_ref[0] = jnp.zeros(inc_ref.shape[1:], F32)
    for w in range(3):
        for l in range(leaves):
            cols = slice(l * LEAF, (l + 1) * LEAF)
            fst_ref[w * leaves + l] = jnp.transpose(fswin_ref[w, :, cols].astype(F32)).astype(BF16)
            rw_ref[w * leaves + l] = rhs_ref[:, cols] if w == 1 else rhswin_ref[w, :, cols]

    def near(lo, hi):
        def body(b, c):
            made = []
            for u in range(UNROLL):
                k = b * UNROLL + u
                t = jnp.clip(np_ref[0, k] - dev * leaves, 0, leaves - 1)
                s = jnp.clip(np_ref[1, k] - (dev - 1) * leaves, 0, 3 * leaves - 1)
                sq = jnp.maximum(dot(fst_ref[s], ftl_ref[t]), 1e-30)
                p = sq * lax.rsqrt(sq)
                tile = ((AMP + (AMP * LN2) * p) * jnp.exp2(-p)).astype(BF16)
                made.append(dot(rw_ref[s], tile))
            for u in range(UNROLL):
                k = b * UNROLL + u
                inc_ref[k + 1] = made[u] + inc_ref[smeta_ref[0, k]]
            return c

        lax.fori_loop(lo // UNROLL, hi // UNROLL, body, 0)

    def copy3(h):
        def copy(i):
            part = pl.ds(h * 64, 64)
            return remote(send3_ref.at[part], recv3_ref.at[g, part], p3_s.at[h, i], p3_r.at[h, i], other_group(i))

        return copy

    def couple(h):
        part = pl.ds(h * 64, 64)
        total = recv2_ref[0, part].astype(F32)
        for o in range(1, groups):
            total = total + recv2_ref[o, part].astype(F32)
        s_ref[part, :] = total
        for i in range(8):
            x = s_ref[pl.ds(h * 64 + i, 8, stride=8), :]
            pr_ref[h * 64 + i * 8 : h * 64 + i * 8 + 8, :] = pack(dot2(unpack(x), ub_ref[i], nt=True))
        made = jnp.concatenate([pr_ref[pl.ds(h * 64 + v, 8, stride=8), :] for v in range(8)], axis=0).astype(BF16)
        send3_ref[part, :] = made
        recv3_ref[g, part] = made
        start(copy3(h), groups)

    def copy4(h):
        def copy(i):
            part = pl.ds(h * 8, 8)
            return remote(
                send4_ref.at[(m + i) % MEMB, part], recv4_ref.at[m, part], p4_s.at[h, i], p4_r.at[h, i], other_member(i)
            )

        return copy

    def descend(h):
        oh3 = oh3_ref[...]
        for b in range(h * 4, h * 4 + 4):
            r = recv3_ref[:, b * 16 : (b + 1) * 16, :].reshape(groups * 16, 128)
            tabd_ref[b * 2 * ROWS : (b + 1) * 2 * ROWS, :] = dot(oh3, r)

        def summed(c):
            return unpack(tabd_ref[pl.ds(h * 8 * ROWS + c, 8, stride=ROWS), :])

        at = used - 1
        down = summed(at)
        while at > 2 * MEMB - 2:
            at -= 1
            down = summed(at) + dot2(down, eg_ref[at], nt=True)
        current = [down]
        breadth = 2
        while breadth <= MEMB:
            at = 2 * MEMB - 2 * breadth
            current = [summed(at + i) + dot2(current[i // 2], eg_ref[at + i], nt=True) for i in range(breadth)]
            breadth *= 2
        for i in range(MEMB):
            send4_ref[i, h * 8 : h * 8 + 8] = pack(current[i])
        part = pl.ds(h * 8, 8)
        recv4_ref[m, part] = send4_ref[m, part]
        start(copy4(h), MEMB)

    def finish(h):
        part = pl.ds(h * 8, 8)
        total = recv4_ref[0, part]
        for i in range(1, MEMB):
            total = total + recv4_ref[i, part]
        current = [unpack(total)]
        lower, upper = slice(h * 8, h * 8 + 8), slice(16 + h * 8, 24 + h * 8)
        breadth = 2
        while breadth <= leaves:
            at = 2 * leaves - 2 * breadth
            grown = []
            for i in range(breadth):
                last = smeta_ref[3, at + i]
                own = jnp.concatenate([lowbuf_ref[last, lower], lowbuf_ref[last, upper]], axis=0)
                grown.append(own + dot2(current[i // 2], lt_ref[at + i], nt=True))
            current = grown
            breadth *= 2
        for l in range(leaves):
            cols = slice(l * LEAF, (l + 1) * LEAF)
            far = dot2(current[l], basis_ref[:, cols])
            last = smeta_ref[1, l]
            out_ref[lower, cols] = inc_ref[last, lower] + far[:8]
            out_ref[upper, cols] = inc_ref[last, upper] + far[8:]

    near(0, CUT[0])
    await_recv(copy2(0), groups)
    couple(0)
    near(CUT[0], CUT[1])
    await_recv(copy2(1), groups)
    couple(1)
    near(CUT[1], CUT[2])
    await_recv(copy3(0), groups)
    descend(0)
    near(CUT[2], CUT[3])
    await_recv(copy3(1), groups)
    descend(1)

    lowbuf_ref[0] = jnp.zeros(lowbuf_ref.shape[1:], F32)
    made = []
    for k in range(low_dev):
        s = jnp.clip(lp_ref[1, k] - (dev - 1) * low_count, 0, 3 * low_count - 1)
        made.append(dot2(unpack(lowwin_ref[s]), lb_ref[k], nt=True))
    for k in range(low_dev):
        lowbuf_ref[k + 1] = made[k] + lowbuf_ref[smeta_ref[2, k]]
    near(CUT[3], near_cap)

    for h in range(2):
        await_recv(copy4(h), MEMB)
        finish(h)
    for c in halo:
        c.wait_send()
    await_send(copy_req, groups)
    await_send(copy1, MEMB)
    for h in range(2):
        await_send(copy2(h), groups)
        await_send(copy3(h), groups)
        await_send(copy4(h), MEMB)


def on_device(coords, rhs, basis, lt, lp, lb, ut, up, ub, npairs, ncount):
    ndev = lax.axis_size(("grp", "sub"))
    groups = ndev // MEMB
    points = rhs.shape[1]
    leaves = points // LEAF
    low_count = 2 * leaves - 2
    near_cap = npairs.shape[1]
    vm = pl.BlockSpec(memory_space=pltpu.VMEM)
    anym = pl.BlockSpec(memory_space=pl.ANY)
    dma = pltpu.SemaphoreType.DMA
    ut = jnp.transpose(ut, (1, 2, 0))
    return pl.pallas_call(
        lambda *refs: kernel(groups, *refs),
        out_shape=jax.ShapeDtypeStruct((32, points), F32),
        in_specs=[anym] * 11,
        out_specs=vm,
        scratch_shapes=[
            pltpu.VMEM(rhs.shape, BF16),
            pltpu.VMEM(basis.shape, BF16),
            pltpu.VMEM(lt.shape, BF16),
            pltpu.VMEM(coords.shape, BF16),
            pltpu.VMEM(up.shape, jnp.int32),
            pltpu.VMEM(npairs.shape, jnp.int32),
            pltpu.VMEM(lp.shape, jnp.int32),
            pltpu.VMEM((1, 1), jnp.int32),
            pltpu.SMEM(npairs.shape, jnp.int32),
            pltpu.SMEM(lp.shape, jnp.int32),
            pltpu.VMEM(ut.shape, BF16),
            pltpu.VMEM(ub.shape, BF16),
            pltpu.VMEM(lb.shape, BF16),
            pltpu.VMEM((32 * ROWS, 128), F32),
            pltpu.VMEM((ROWS, 64, 64), BF16),
            pltpu.VMEM((8, 128), jnp.int32),
            pltpu.SMEM((8, 128), jnp.int32),
            pltpu.VMEM((3 * low_count, 16, 128), F32),
            pltpu.VMEM((3, 16, points), BF16),
            pltpu.VMEM((3, 32, points), BF16),
            pltpu.VMEM((leaves, 16, LEAF), BF16),
            pltpu.VMEM((3 * leaves, LEAF, 16), BF16),
            pltpu.VMEM((3 * leaves, 32, LEAF), BF16),
            pltpu.VMEM((near_cap + 1, 32, LEAF), F32),
            pltpu.VMEM((lp.shape[1] + 1, 32, 64), F32),
            pltpu.VMEM((groups, 8, 128), jnp.int32),
            pltpu.VMEM((MEMB, 16, 128), BF16),
            pltpu.VMEM((2, ROWS * 8, 128), F32),
            pltpu.VMEM((groups, 128, 128), BF16),
            pltpu.VMEM((groups, 128, 128), BF16),
            pltpu.VMEM((128, 128), F32),
            pltpu.VMEM((128, 128), F32),
            pltpu.VMEM((128, 128), BF16),
            pltpu.VMEM((groups, 128, 128), BF16),
            pltpu.VMEM((8 * 2 * ROWS, 128), F32),
            pltpu.VMEM((MEMB, 16, 128), F32),
            pltpu.VMEM((MEMB, 16, 128), F32),
            pltpu.VMEM((2 * ROWS, groups * 16), BF16),
            dma((14,)),
            dma((6,)),
            dma((6,)),
            dma((groups,)),
            dma((groups,)),
            dma((MEMB,)),
            dma((MEMB,)),
            dma((2, groups)),
            dma((2, groups)),
            dma((2, groups)),
            dma((2, groups)),
            dma((2, MEMB)),
            dma((2, MEMB)),
        ],
        compiler_params=pltpu.CompilerParams(
            collective_id=0, has_side_effects=True, vmem_limit_bytes=56 * 2**20
        ),
        name="tree_product",
    )(coords, rhs, basis, lt, up, npairs, lp, ncount.reshape(1, 1), ut, ub, lb)


def solution(mesh):
    both = ("grp", "sub")
    in_specs = (
        P(None, both), P(None, both), P(None, both), P(both), P(None, both), P(both),
        P(), P(None, both), P(both), P(None, both), P(both),
    )
    return jax.shard_map(on_device, mesh=mesh, in_specs=in_specs, out_specs=P(None, both), check_vma=False)
```
